32 devices in a mesh: fsdp: 4 (over y, x), ctx: 8 (over z, core).
Axes of the slice: x: 2, y: 2, z: 4, core: 2. Of those that a mesh axis runs over, the one named last changes fastest.
Arguments:
- hidden_in: bfloat16 [8, 1024, 2048], P('fsdp', 'ctx'), may hold values from -6 to 6
- positions: int32 [8, 1024], P('fsdp', 'ctx'), may hold values from 0 to 1023, as said below
- cotangent: bfloat16 [8, 1024, 2048], P('fsdp', 'ctx'), may hold values from -6 to 6
- norm_gain: bfloat16 [2048], P('fsdp'), may hold values from 0.5 to 1.5
- w_query: bfloat16 [2048, 2048], P('fsdp'), may hold values from -0.125 to 0.125
- w_key: bfloat16 [2048, 256], P('fsdp'), may hold values from -0.125 to 0.125
- w_value: bfloat16 [2048, 256], P('fsdp'), may hold values from -0.125 to 0.125
- w_out: bfloat16 [2048, 2048], P('fsdp'), may hold values from -2 to 2
- ffn_gain: bfloat16 [2048], P('fsdp'), may hold values from 0.5 to 1.5
- w_gate: bfloat16 [2048, 5632], P('fsdp'), may hold values from -0.125 to 0.125
- w_up: bfloat16 [2048, 5632], P('fsdp'), may hold values from -0.125 to 0.125
- w_down: bfloat16 [5632, 2048], P('fsdp'), may hold values from -0.078125 to 0.078125
Outputs:
- output: bfloat16 [8, 1024, 2048], P('fsdp', 'ctx')
- grad_in: float32 [8, 1024, 2048], P('fsdp', 'ctx')
- grad_norm_gain: float32 [2048], P('fsdp')
- grad_query: float32 [2048, 2048], P('fsdp')
- grad_key: float32 [2048, 256], P('fsdp')
- grad_value: float32 [2048, 256], P('fsdp')
- grad_out: float32 [2048, 2048], P('fsdp')
- grad_ffn_gain: float32 [2048], P('fsdp')
- grad_gate: float32 [2048, 5632], P('fsdp')
- grad_up: float32 [2048, 5632], P('fsdp')
- grad_down: float32 [5632, 2048], P('fsdp')
The draws below stay inside these ranges and needn't reach their ends.
Inputs may be any that keep to these rules, and one draw needn't show every extreme that they name: In each sequence, the 128 tokens that one device of ctx holds are consecutive positions in increasing order, starting at a multiple of 128; the devices of ctx hold different such runs, in an order drawn for each sequence.
All inputs are finite; a program needn't handle non-finite values.
Results may differ from the reference program's by a relative error of at most 0.023.
Values may be sent and summed in bfloat16 or wider, within the bound.
No kernel may reach another device: no remote copies, remote signals or barrier semaphores. Data moves between devices by JAX's collectives and lax.ppermute only.
A program may use at most 704 MiB of HBM per device.

```python
import jax
import jax.numpy as jnp
from jax import lax

D = 2048
H = 32
KVH = 4
HD = 64
FF = 5632
TOK_SEQ = 128
LEN = 1024
SEQS = 8


def draw_positions(key, part):
    key = jax.random.fold_in(key, 7)
    run_count = LEN // TOK_SEQ
    seq_keys = jax.random.split(key, SEQS)
    order = jax.vmap(lambda seq_key: jax.random.permutation(seq_key, run_count))(seq_keys)
    inside = jnp.arange(TOK_SEQ, dtype=jnp.int32)
    placed = order.astype(jnp.int32)[:, :, None] * TOK_SEQ + inside[None, None, :]
    return placed.reshape(SEQS, LEN).astype(jnp.int32)


def level_of(stream_key, shape, cuts, low, top_value):
    gain = 1.0
    for dim, blocks in cuts:
        steps = jax.random.uniform(jax.random.fold_in(jax.random.fold_in(stream_key, 6), dim), (blocks,), jnp.float32, low / len(cuts), top_value / len(cuts))
        gain = gain * jnp.repeat(jnp.exp(steps), shape[dim] // blocks).reshape((-1,) + (1,) * (len(shape) - 1 - dim))
    return gain


def gaussian(rng, dims, scale, limit, shards=(), kind=jnp.bfloat16):
    gain = level_of(rng, dims, shards, -0.22, 0.18) if shards else 1.0
    entries = jax.random.normal(rng, dims, jnp.float32) * scale * gain
    return jnp.minimum(jnp.maximum(entries, -limit), limit).astype(kind)


def setup_inputs(seed: int = 0) -> dict:
    arg_keys = jax.random.split(jax.random.key(seed), 13)
    return {
        "hidden_in": gaussian(arg_keys[0], (SEQS, LEN, D), 1.0, 6.0, ((0, 4), (1, 8))),
        "positions": draw_positions(jax.random.fold_in(arg_keys[12], 71), 0),
        "cotangent": gaussian(arg_keys[2], (SEQS, LEN, D), 1.0, 6.0, ((0, 4), (1, 8))),
        "norm_gain": jnp.clip(1.0 + 0.1 * jax.random.normal(arg_keys[3], (D,), jnp.float32), 0.5, 1.5).astype(jnp.bfloat16),
        "w_query": gaussian(arg_keys[4], (D, H * HD), D ** -0.5, 0.125, ((0, 4),)),
        "w_key": gaussian(arg_keys[5], (D, KVH * HD), D ** -0.5, 0.125, ((0, 4),)),
        "w_value": gaussian(arg_keys[6], (D, KVH * HD), D ** -0.5, 0.125, ((0, 4),)),
        "w_out": gaussian(arg_keys[7], (H * HD, D), 8 ** -0.5, 2.0, ((0, 4),)),
        "ffn_gain": jnp.clip(1.0 + 0.1 * jax.random.normal(arg_keys[8], (D,), jnp.float32), 0.5, 1.5).astype(jnp.bfloat16),
        "w_gate": gaussian(arg_keys[9], (D, FF), D ** -0.5, 0.125, ((0, 4),)),
        "w_up": gaussian(arg_keys[10], (D, FF), D ** -0.5, 0.125, ((0, 4),)),
        "w_down": gaussian(arg_keys[11], (FF, D), FF ** -0.5, 0.078125, ((0, 4),)),
    }


NORM_EPS = 1e-05
MASKED = -1e+30
HIGHEST = lax.Precision.HIGHEST

@jax.custom_vjp
def low(v):
    return lax.optimization_barrier(v.astype(jnp.bfloat16)).astype(jnp.float32)

@jax.custom_vjp
def low_back(v):
    return v

def low_keep(v):
    return (low(v), None)

def low_pass(kept, grad):
    return (grad,)

def back_keep(v):
    return (v, None)

def back_low(kept, grad):
    return (low(grad),)
low.defvjp(low_keep, low_pass)
low_back.defvjp(back_keep, back_low)

def norm_rows(inputs, gain_row):
    row_scale = lax.rsqrt(lax.optimization_barrier(jnp.mean(inputs * inputs, -1, keepdims=True)) + NORM_EPS)
    return inputs * row_scale * gain_row

def rope_table(positions):
    half_width = HD // 2
    spread = 10000.0 ** (-jnp.arange(half_width, dtype=jnp.float32) / half_width)
    turned = positions.astype(jnp.float32)[:, None] * spread[None, :]
    return (jnp.cos(turned)[:, None, :], jnp.sin(turned)[:, None, :])

def rotate(inputs, cosine, sine_table):
    half_width = inputs.shape[-1] // 2
    first_half = inputs[..., :half_width]
    second_half = inputs[..., half_width:]
    return jnp.concatenate([first_half * cosine - second_half * sine_table, first_half * sine_table + second_half * cosine], -1)

def attend_block(queries, query_pos, key_rows, values, key_pos):
    score_scale = queries.shape[-1] ** (-0.5)
    scores = low_back(jnp.einsum('bkgd,lkd->kgbl', queries, key_rows, precision=HIGHEST) * score_scale)
    allowed = key_pos[None, None, None, :] <= query_pos[None, None, :, None]
    weights = jax.nn.softmax(jnp.where(allowed, scores, MASKED), axis=-1)
    return jnp.einsum('kgbl,lkd->bkgd', low(weights), values, precision=HIGHEST)

def layer(inputs, positions, weight_set):
    gain_one, query_w, key_w, value_w, out_w, gain_two, gate_w, up_w, down_w = weight_set
    seq_len = inputs.shape[0]
    group_size = H // KVH
    normed_one = low(norm_rows(inputs, gain_one))
    query_raw = low_back(jnp.dot(normed_one, query_w, precision=HIGHEST)).reshape(seq_len, H, HD)
    key_raw = low_back(jnp.dot(normed_one, key_w, precision=HIGHEST)).reshape(seq_len, KVH, HD)
    values = low(low_back(jnp.dot(normed_one, value_w, precision=HIGHEST))).reshape(seq_len, KVH, HD)
    cosine, sine_table = rope_table(positions)
    queries = low(rotate(query_raw, cosine, sine_table)).reshape(seq_len, KVH, group_size, HD)
    key_rows = low(rotate(key_raw, cosine, sine_table))
    block_rows = min(512, seq_len)
    block_count = seq_len // block_rows
    checked = jax.checkpoint(attend_block)
    mixture = lax.map(lambda block_pair: checked(block_pair[0], block_pair[1], key_rows, values, positions), (queries.reshape(block_count, block_rows, KVH, group_size, HD), positions.reshape(block_count, block_rows)))
    attended = low(low_back(mixture.reshape(seq_len, H * HD)))
    residual = inputs + low_back(jnp.dot(attended, out_w, precision=HIGHEST))
    normed_two = low(norm_rows(residual, gain_two))
    gate_proj = low_back(jnp.dot(normed_two, gate_w, precision=HIGHEST))
    up_proj = low_back(jnp.dot(normed_two, up_w, precision=HIGHEST))
    hidden = low(jax.nn.silu(gate_proj) * up_proj)
    return residual + low_back(jnp.dot(hidden, down_w, precision=HIGHEST))

def reference(hidden_in, positions, cotangent, norm_gain, w_query, w_key, w_value, w_out, ffn_gain, w_gate, w_up, w_down):
    weight_set = (norm_gain.astype(jnp.float32), w_query.astype(jnp.float32), w_key.astype(jnp.float32), w_value.astype(jnp.float32), w_out.astype(jnp.float32), ffn_gain.astype(jnp.float32), w_gate.astype(jnp.float32), w_up.astype(jnp.float32), w_down.astype(jnp.float32))
    checked_layer = jax.checkpoint(layer)

    def forward(inputs, weight_tuple):
        return lax.map(lambda seq_pair: checked_layer(seq_pair[0], seq_pair[1], weight_tuple), (inputs, positions))
    output, pullback = jax.vjp(forward, hidden_in.astype(jnp.float32), weight_set)
    grad_in, grad_set = pullback(cotangent.astype(jnp.float32))
    return (output.astype(jnp.bfloat16), grad_in, grad_set[0], grad_set[1], grad_set[2], grad_set[3], grad_set[4], grad_set[5], grad_set[6], grad_set[7], grad_set[8])
```

```python
import jax
import jax.numpy as jnp
from jax import lax
from jax.sharding import PartitionSpec as P

H = 32
KVH = 4
HD = 64


NORM_EPS = 1e-05
MASKED = -1e30


def rms_scale(inputs):
    return lax.rsqrt(jnp.mean(inputs * inputs, -1, keepdims=True) + NORM_EPS)


def rope_table(positions):
    half_width = HD // 2
    spread = 10000.0 ** (-jnp.arange(half_width, dtype=jnp.float32) / half_width)
    turned = positions.astype(jnp.float32)[..., None] * spread
    return (jnp.cos(turned)[..., None, :], jnp.sin(turned)[..., None, :])


def rotate(inputs, cosine, sine_table):
    half_width = inputs.shape[-1] // 2
    first_half = inputs[..., :half_width]
    second_half = inputs[..., half_width:]
    return jnp.concatenate(
        [
            first_half * cosine - second_half * sine_table,
            first_half * sine_table + second_half * cosine,
        ],
        -1,
    )


def norm_back(grad_normed, inputs, row_scale, gain_row):
    scaled_grad = grad_normed * gain_row
    grad_gain = jnp.sum(grad_normed * inputs * row_scale, 0)
    grad_inputs = row_scale * scaled_grad - inputs * row_scale**3 * jnp.mean(
        scaled_grad * inputs, -1, keepdims=True
    )
    return (grad_inputs, grad_gain)


def item_scores(queries, key_rows, query_pos, key_pos):
    score_scale = queries.shape[-1] ** (-0.5)
    scores = (
        jnp.einsum("tgd,nd->gtn", queries, key_rows, preferred_element_type=jnp.float32)
        * score_scale
    )
    allowed = key_pos[None, None, :] <= query_pos[None, :, None]
    return jnp.where(allowed, scores, MASKED)


def attend_item(operands):
    queries, key_rows, values, query_pos, key_pos = operands
    scores = item_scores(queries, key_rows, query_pos, key_pos)
    row_top = jnp.max(scores, -1, keepdims=True)
    weights = jnp.exp(scores - row_top)
    row_total = jnp.sum(weights, -1, keepdims=True)
    shares = weights / row_total
    mixture = jnp.einsum(
        "gtn,nd->tgd", shares.astype(jnp.bfloat16), values, preferred_element_type=jnp.float32
    )
    return (mixture, (row_top + jnp.log(row_total))[..., 0])


def attend_back_item(operands):
    queries, key_rows, values, query_pos, key_pos, log_total, grad_mixture = operands
    score_scale = queries.shape[-1] ** (-0.5)
    scores = item_scores(queries, key_rows, query_pos, key_pos)
    shares = jnp.exp(scores - log_total[..., None])
    grad_shares = jnp.einsum(
        "tgd,nd->gtn", grad_mixture, values, preferred_element_type=jnp.float32
    )
    inner_sum = jnp.sum(shares * grad_shares, -1, keepdims=True)
    grad_scores = (shares * (grad_shares - inner_sum)).astype(jnp.bfloat16)
    grad_queries = (
        jnp.einsum("gtn,nd->tgd", grad_scores, key_rows, preferred_element_type=jnp.float32)
        * score_scale
    )
    grad_keys = (
        jnp.einsum("gtn,tgd->nd", grad_scores, queries, preferred_element_type=jnp.float32)
        * score_scale
    )
    grad_values = jnp.einsum(
        "gtn,tgd->nd", shares.astype(jnp.bfloat16), grad_mixture, preferred_element_type=jnp.float32
    )
    return (grad_queries, grad_keys, grad_values)


def to_items(array, seq_count, tok_count, group_size):
    shaped = array.reshape(seq_count, tok_count, KVH, group_size, HD).transpose(0, 2, 1, 3, 4)
    return shaped.reshape(seq_count * KVH, tok_count, group_size, HD)


def from_items(array, seq_count, tok_count, group_size):
    shaped = array.reshape(seq_count, KVH, tok_count, group_size, HD).transpose(0, 2, 1, 3, 4)
    return shaped.reshape(seq_count, tok_count, H, HD)


def at(array, start, size, axis=0):
    return lax.dynamic_slice_in_dim(array, start, size, axis)


def on_device(
    hidden_in,
    positions,
    cotangent,
    norm_gain,
    w_query,
    w_key,
    w_value,
    w_out,
    ffn_gain,
    w_gate,
    w_up,
    w_down,
):
    bf, f32 = jnp.bfloat16, jnp.float32
    seq_count, tok_count, model_width = hidden_in.shape
    row_count = seq_count * tok_count
    group_size = H // KVH
    parts = lax.axis_size("fsdp")
    runs = lax.axis_size("ctx")
    levels = runs // 2
    mine = lax.axis_index("fsdp")
    run = lax.axis_index("ctx")
    core = lax.rem(run, 2)
    level = run // 2
    shard = model_width // parts
    ff_part = w_down.shape[0]

    def hop(array, bit):
        return lax.ppermute(array, "fsdp", [(i, i ^ bit) for i in range(parts)])

    def swap_core(array):
        return lax.ppermute(array, "ctx", [(i, i ^ 1) for i in range(runs)])

    def level_send(array, pairs):
        return lax.ppermute(
            array, "ctx", [(2 * a + k, 2 * b + k) for a, b in pairs for k in range(2)]
        )

    def spread(local):
        if parts != 4:
            return [hop(local, bit) for bit in range(1, parts)]
        half = local.shape[0] // 2
        from_x, from_y = hop(local, 1), hop(local, 2)
        return [from_x, from_y, hop(from_x[:half], 2), hop(from_y[half:], 1)]

    def gather_rows(local):
        rows, cols = local.shape
        half = rows // 2
        own = at(local, core * half, half)
        got = jnp.concatenate(spread(own), 0)
        other = swap_core(got)
        whole = jnp.zeros((parts, 2, half, cols), local.dtype)
        whole = lax.dynamic_update_slice(
            whole, local.reshape(1, 2, half, cols), (mine, 0, 0, 0)
        )
        for step in range(1, parts):
            for source, side in ((got, core), (other, 1 - core)):
                piece = source[(step - 1) * half : step * half].reshape(1, 1, half, cols)
                whole = lax.dynamic_update_slice(whole, piece, (mine ^ step, side, 0, 0))
        return whole.reshape(parts * rows, cols)

    def gather_columns(locals_, cols):
        rows = locals_[0].shape[0]
        half = rows // 2

        def block(index, start, size):
            return jnp.concatenate(
                [
                    lax.dynamic_slice(a, (start, index * cols), (size, cols))
                    for a in locals_
                ],
                1,
            )

        width = cols * len(locals_)
        got = jnp.concatenate(
            [hop(block(mine ^ bit, core * half, half), bit) for bit in range(1, parts)],
            0,
        )
        other = swap_core(got)
        whole = jnp.zeros((parts, 2, half, width), locals_[0].dtype)
        whole = lax.dynamic_update_slice(
            whole, block(mine, 0, rows).reshape(1, 2, half, width), (mine, 0, 0, 0)
        )
        for step in range(1, parts):
            for source, side in ((got, core), (other, 1 - core)):
                piece = source[(step - 1) * half : step * half].reshape(1, 1, half, width)
                whole = lax.dynamic_update_slice(whole, piece, (mine ^ step, side, 0, 0))
        return whole.reshape(parts * rows, width)

    def gather_tokens(local):
        return jnp.concatenate([local] + spread(local), 0)

    def sum_blocks(blocks):
        if parts != 4:
            return sum(
                [hop(blocks[bit], bit).astype(f32) for bit in range(1, parts)],
                blocks[0].astype(f32),
            )
        half = blocks[0].shape[0] // 2
        low_part = hop(blocks[3][half:], 1)
        top_part = hop(blocks[3][:half], 2)
        add = lambda a, b: (a.astype(f32) + b.astype(f32)).astype(bf)
        to_x = jnp.concatenate([add(blocks[1][:half], top_part), blocks[1][half:]], 0)
        to_y = jnp.concatenate([blocks[2][:half], add(blocks[2][half:], low_part)], 0)
        from_x, from_y = hop(to_x, 1), hop(to_y, 2)
        return blocks[0].astype(f32) + from_x.astype(f32) + from_y.astype(f32)

    def sum_levels(local):
        add = lambda a, b: (a.astype(f32) + b.astype(f32)).astype(bf)
        middle = levels // 2
        last = levels - 1
        total = local
        for step in range(middle - 1):
            total = add(
                total, level_send(total, [(step, step + 1), (last - step, last - step - 1)])
            )
        total = add(total, level_send(total, [(middle - 1, middle), (middle, middle - 1)]))
        for step in reversed(range(middle - 1)):
            got = level_send(total, [(step + 1, step), (last - step - 1, last - step)])
            total = jnp.where((level == step) | (level == last - step), got, total)
        return total

    def both_halves(local, axis=0):
        other = swap_core(local)
        first = jnp.where(core == 0, local, other)
        second = jnp.where(core == 0, other, local)
        return jnp.concatenate([first, second], axis).astype(f32)

    def pair_sum(array, axis):
        size = array.shape[axis] // 2
        got = swap_core(at(array, (1 - core) * size, size, axis))
        kept = at(array, core * size, size, axis)
        return (kept.astype(f32) + got.astype(f32)).astype(bf)

    def reduce_rows(partial):
        cols = partial.shape[1]
        half = shard // 2
        split = pair_sum(partial.reshape(parts, shard, cols), 1)
        blocks = [at(split, mine ^ step, 1).reshape(half, cols) for step in range(parts)]
        return both_halves(sum_levels(sum_blocks(blocks).astype(bf)))

    def reduce_columns(partial):
        cols = partial.shape[1]
        half = shard // 2
        split = pair_sum(partial.reshape(parts, shard, cols), 1)
        blocks = [at(split, mine ^ step, 1).reshape(half, cols) for step in range(parts)]
        got = [blocks[0]] + [hop(blocks[step], step) for step in range(1, parts)]
        whole = jnp.zeros((parts, half, cols), bf)
        for step in range(parts):
            whole = lax.dynamic_update_slice(whole, got[step][None], (mine ^ step, 0, 0))
        return whole

    dot = lambda a, b: jnp.dot(a, b, preferred_element_type=f32)

    gains = lax.all_gather(jnp.stack([norm_gain, ffn_gain], 0), "fsdp", axis=1, tiled=True)
    gain_one, gain_two = gains[0].astype(f32), gains[1].astype(f32)
    key_value_w = gather_rows(jnp.concatenate([w_key, w_value], 1))
    query_w = gather_rows(w_query)
    out_w = gather_rows(w_out)
    wide_w = gather_columns([w_gate, w_up], ff_part)
    grad_y_low = cotangent.reshape(row_count, model_width)
    all_dm = gather_tokens(grad_y_low)

    inputs = hidden_in.astype(f32).reshape(row_count, model_width)
    scale_one = rms_scale(inputs)
    normed_one = (inputs * scale_one * gain_one).astype(bf)
    key_value = dot(normed_one, key_value_w)
    cosine, sine_table = rope_table(positions)
    keys_low = rotate(
        key_value[:, : KVH * HD].reshape(seq_count, tok_count, KVH, HD), cosine, sine_table
    ).astype(bf)
    packed = jnp.concatenate(
        [
            keys_low.reshape(seq_count, tok_count, KVH * HD),
            key_value[:, KVH * HD :].astype(bf).reshape(seq_count, tok_count, KVH * HD),
        ],
        -1,
    )
    all_packed = lax.all_gather(packed, "ctx", axis=1, tiled=True)
    all_keys, all_values = all_packed[..., : KVH * HD], all_packed[..., KVH * HD :]
    all_pos = lax.all_gather(positions, "ctx", axis=1, tiled=True)
    query_low = rotate(
        dot(normed_one, query_w).reshape(seq_count, tok_count, H, HD), cosine, sine_table
    ).astype(bf)
    full_len = all_keys.shape[1]
    item_query = to_items(query_low, seq_count, tok_count, group_size)
    item_keys = (
        all_keys.reshape(seq_count, full_len, KVH, HD)
        .transpose(0, 2, 1, 3)
        .reshape(seq_count * KVH, full_len, HD)
    )
    item_values = (
        all_values.reshape(seq_count, full_len, KVH, HD)
        .transpose(0, 2, 1, 3)
        .reshape(seq_count * KVH, full_len, HD)
    )
    item_qpos = jnp.repeat(positions, KVH, axis=0)
    item_kpos = jnp.repeat(all_pos, KVH, axis=0)
    mixture_items, log_total = lax.map(
        attend_item, (item_query, item_keys, item_values, item_qpos, item_kpos)
    )
    attended = (
        from_items(mixture_items, seq_count, tok_count, group_size)
        .reshape(row_count, H * HD)
        .astype(bf)
    )
    residual = inputs + dot(attended, out_w)
    scale_two = rms_scale(residual)
    normed_two = (residual * scale_two * gain_two).astype(bf)
    all_normed = gather_tokens(normed_two)

    gate_w, up_w = wide_w[:, :ff_part], wide_w[:, ff_part:]
    gate_proj, up_proj = dot(all_normed, gate_w), dot(all_normed, up_w)
    sigmoid_gate = jax.nn.sigmoid(gate_proj)
    hidden_low = (gate_proj * sigmoid_gate * up_proj).astype(bf)
    grad_hidden = dot(all_dm, w_down.T)
    grad_down_part = dot(hidden_low.T, all_dm).astype(bf)
    grad_down = both_halves(sum_levels(pair_sum(grad_down_part, 0)))
    grad_up_in = (grad_hidden * gate_proj * sigmoid_gate).astype(bf)
    grad_gate_in = (
        grad_hidden * up_proj * sigmoid_gate * (1.0 + gate_proj * (1.0 - sigmoid_gate))
    ).astype(bf)
    grad_wide_in = jnp.concatenate([grad_gate_in, grad_up_in], 1)
    grad_normed_part = dot(grad_wide_in, wide_w.T).astype(bf)
    split_rows = lambda a: [a[i * row_count : (i + 1) * row_count] for i in range(parts)]
    grad_normed_two = sum_blocks(split_rows(grad_normed_part))
    grad_wide_part = dot(all_normed.T, grad_wide_in).astype(bf)
    wide_blocks = reduce_columns(grad_wide_part)
    wide_sum = sum_levels(wide_blocks)
    half_rows = lambda a: both_halves(
        a.transpose(1, 0, 2).reshape(shard // 2, parts * ff_part)
    )
    grad_gate_w = half_rows(wide_sum[:, :, :ff_part])
    grad_up_w = half_rows(wide_sum[:, :, ff_part:])

    grad_y = grad_y_low.astype(f32)
    grad_res_norm, grad_gain_two = norm_back(grad_normed_two, residual, scale_two, gain_two)
    grad_residual = grad_y + grad_res_norm
    grad_proj = grad_residual.astype(bf)
    grad_out_w = reduce_rows(dot(attended.T, grad_proj).astype(bf))
    grad_attended = dot(grad_proj, out_w.T).astype(bf)
    mixed_part = dot(hidden_low, w_down).astype(bf)
    output = (
        (residual + sum_blocks(split_rows(mixed_part)))
        .astype(bf)
        .reshape(seq_count, tok_count, model_width)
    )

    item_grad = to_items(grad_attended, seq_count, tok_count, group_size)
    grad_q_items, grad_k_items, grad_v_items = lax.map(
        attend_back_item,
        (item_query, item_keys, item_values, item_qpos, item_kpos, log_total, item_grad),
    )
    by_run = lambda a: a.reshape(seq_count, KVH, levels, 2, tok_count, HD)
    grad_kv = jnp.stack([by_run(grad_k_items), by_run(grad_v_items)], 0).astype(bf)
    grad_kv = grad_kv.transpose(3, 4, 0, 1, 2, 5, 6)
    kept = at(grad_kv, core, 1, 1)[:, 0].astype(f32)
    got = swap_core(at(grad_kv, 1 - core, 1, 1)[:, 0])
    by_level = kept + got.astype(f32)
    own_kv = at(by_level, level, 1)[0]
    for step in range(1, levels):
        sent = at(by_level, lax.rem(level + step, levels), 1)[0].astype(bf)
        own_kv = own_kv + level_send(
            sent, [(i, (i + step) % levels) for i in range(levels)]
        ).astype(f32)
    grad_keys_low = (
        rotate(own_kv[0].transpose(0, 2, 1, 3), cosine, -sine_table)
        .astype(bf)
        .reshape(row_count, KVH * HD)
    )
    grad_values_low = own_kv[1].transpose(0, 2, 1, 3).reshape(row_count, KVH * HD).astype(bf)
    grad_query_rot = from_items(grad_q_items, seq_count, tok_count, group_size)
    grad_query_low = (
        rotate(grad_query_rot, cosine, -sine_table).astype(bf).reshape(row_count, H * HD)
    )
    grad_kv_low = jnp.concatenate([grad_keys_low, grad_values_low], 1)
    grad_query_w = reduce_rows(dot(normed_one.T, grad_query_low).astype(bf))
    grad_kv_w = reduce_rows(dot(normed_one.T, grad_kv_low).astype(bf))
    grad_normed_one = dot(grad_query_low, query_w.T) + dot(grad_kv_low, key_value_w.T)
    grad_in_norm, grad_gain_one = norm_back(grad_normed_one, inputs, scale_one, gain_one)
    grad_in = (grad_residual + grad_in_norm).reshape(seq_count, tok_count, model_width)
    gain_sum = lax.psum(jnp.stack([grad_gain_one, grad_gain_two], 0), ("fsdp", "ctx"))
    gain_own = at(gain_sum, mine * shard, shard, 1)
    return (
        output,
        grad_in,
        gain_own[0],
        grad_query_w,
        grad_kv_w[:, : KVH * HD],
        grad_kv_w[:, KVH * HD :],
        grad_out_w,
        gain_own[1],
        grad_gate_w,
        grad_up_w,
        grad_down,
    )


def solution(mesh):
    placed = (
        P("fsdp", "ctx", None),
        P("fsdp", "ctx"),
        P("fsdp", "ctx", None),
        P("fsdp"),
        P("fsdp", None),
        P("fsdp", None),
        P("fsdp", None),
        P("fsdp", None),
        P("fsdp"),
        P("fsdp", None),
        P("fsdp", None),
        P("fsdp", None),
    )
    return jax.shard_map(
        on_device,
        mesh=mesh,
        in_specs=placed,
        out_specs=(
            P("fsdp", "ctx", None),
            P("fsdp", "ctx", None),
            P("fsdp"),
            P("fsdp", None),
            P("fsdp", None),
            P("fsdp", None),
            P("fsdp", None),
            P("fsdp"),
            P("fsdp", None),
            P("fsdp", None),
            P("fsdp", None),
        ),
        check_vma=False,
    )
```

```python
import functools

import jax
import jax.numpy as jnp
from jax import lax
from jax.experimental import pallas as pl
from jax.experimental.pallas import tpu as pltpu
from jax.sharding import PartitionSpec as P

H = 32
KVH = 4
HD = 64
GROUP = H // KVH
KW = KVH * HD


NORM_EPS = 1e-05
MASKED = -1e30
BF = jnp.bfloat16
F32 = jnp.float32
ROOM = 60 * 1024 * 1024
EXTRA = 16


def rms_scale(inputs):
    return lax.rsqrt(jnp.mean(inputs * inputs, -1, keepdims=True) + NORM_EPS)


def norm_back(grad_normed, inputs, row_scale, gain_row):
    scaled_grad = grad_normed * gain_row
    grad_gain = jnp.sum(grad_normed * inputs * row_scale, 0)
    grad_inputs = row_scale * scaled_grad - inputs * row_scale**3 * jnp.mean(
        scaled_grad * inputs, -1, keepdims=True
    )
    return (grad_inputs, grad_gain)


def at(array, start, size, axis=0):
    return lax.dynamic_slice_in_dim(array, start, size, axis)


def dot(a, b):
    return jnp.dot(a, b, preferred_element_type=F32)


def dot_cols(a, b):
    return lax.dot_general(a, b, (((1,), (1,)), ((), ())), preferred_element_type=F32)


def dot_rows(a, b):
    return lax.dot_general(a, b, (((0,), (0,)), ((), ())), preferred_element_type=F32)


def swap_halves(value):
    lane = lax.broadcasted_iota(jnp.int32, value.shape, 1)
    size = value.shape[1]
    ahead = pltpu.roll(value, size - HD // 2, 1)
    behind = pltpu.roll(value, HD // 2, 1)
    return jnp.where(lane % HD < HD // 2, ahead, behind)


def spin(value, cosine, sine):
    return value * cosine + swap_halves(value) * sine


def call(
    body, outs, args, scratch=(), flops=0, nbytes=0, grid=None, in_specs=None, out_specs=None,
    after=(), prefetch=False,
):
    whole = pl.BlockSpec(memory_space=pltpu.VMEM)
    many = isinstance(outs, (list, tuple))
    in_specs = list(in_specs or [whole] * len(args))
    count = len(args)
    args = [*args, *after]
    in_specs += [pl.BlockSpec(memory_space=pl.ANY)] * len(after)

    def run(*refs):
        return body(*refs[:count], *refs[count + len(after) :])

    options = pltpu.CompilerParams(vmem_limit_bytes=ROOM)
    cost = pl.CostEstimate(flops=flops, bytes_accessed=nbytes, transcendentals=0)
    if prefetch:
        return pl.pallas_call(
            run,
            out_shape=outs,
            grid_spec=pltpu.PrefetchScalarGridSpec(
                num_scalar_prefetch=1, grid=grid, in_specs=in_specs, out_specs=out_specs
            ),
            compiler_params=options,
            cost_estimate=cost,
        )(*args)
    return pl.pallas_call(
        run,
        out_shape=outs,
        in_specs=in_specs,
        out_specs=out_specs or ([whole] * len(outs) if many else whole),
        scratch_shapes=list(scratch),
        grid=grid or (),
        compiler_params=options,
        cost_estimate=cost,
    )(*args)


def shape(dims, kind):
    return jax.ShapeDtypeStruct(tuple(dims), kind)


class Pieces:
    def __init__(self, own, sources, blocks, cell, width, levels=0):
        self.levels = levels
        self.own, self.sources, self.blocks = list(own), list(sources), tuple(blocks)
        self.cell, self.width = cell, width
        self.part_rows = own[0].shape[0]
        self.count = len(self.own) + len(self.sources)
        self.copies = len(self.own) + len(self.blocks)

    def args(self):
        return self.own + self.sources

    def spot(self, where, step, flip):
        side = where[2] ^ flip
        if self.levels:
            side = lax.rem(where[3] + self.levels - step, self.levels) * 2 + side
        return pl.multiple_of(side * self.cell, self.cell)

    def moves(self, where, refs, bit, first, size):
        own, sources = refs[: len(self.own)], refs[len(self.own) :]
        step = self.width // len(self.own)
        moves = []
        if bit == 0:
            for number, source in enumerate(own):
                column = first
                if len(own) > 1:
                    column = pl.multiple_of(where[0] * step + first, 128)
                moves.append((source.at[:, pl.ds(column, size)], 0, self.part_rows, number))
        for source, row, step_, flip, flag in self.blocks:
            if flag != bit:
                continue
            spot = self.spot(where, step_, flip)
            for number in range(len(own)):
                place = sources[source].at[pl.ds(row, self.cell), pl.ds(number * step + first, size)]
                moves.append((place, spot, self.cell, number))
        return moves

    def whole_moves(self, where, refs, bit):
        own, sources = refs[: len(self.own)], refs[len(self.own) :]
        step = self.width // len(self.own)
        moves = []
        if bit == 0:
            for number, source in enumerate(own):
                column = pl.multiple_of(where[0] * step, 128) if len(own) > 1 else 0
                moves.append(
                    (source.at[:, pl.ds(column, step)], 0, self.part_rows, number * step, step)
                )
        for source, row, step_, flip, flag in self.blocks:
            if flag == bit:
                spot = self.spot(where, step_, flip)
                moves.append(
                    (sources[source].at[pl.ds(row, self.cell), :], spot, self.cell, 0, self.width)
                )
        return moves


def fetch_parts(pieces, where, refs, held, sems, parts):
    groups, number = [], 0
    for bit in range(parts):
        group = []
        for source, row, rows, column, cols in pieces.whole_moves(where, refs, bit):
            target = held.at[bit, pl.ds(row, rows), pl.ds(column, cols)]
            copy = pltpu.make_async_copy(source, target, sems.at[number])
            copy.start()
            group.append(copy)
            number += 1
        groups.append(group)
    return groups


SMEM = pl.BlockSpec(memory_space=pltpu.SMEM)
VMEM = pl.BlockSpec(memory_space=pltpu.VMEM)
HBM = pl.BlockSpec(memory_space=pl.ANY)


def forward_body(pieces, parts, where, left_ref, *refs):
    (out_ref, held, sems), refs = refs[-3:], refs[:-3]
    groups = fetch_parts(pieces, where, refs, held, sems, parts)
    rows = pieces.part_rows
    chunk = min(512, pieces.width)
    for bit in range(parts):
        for copy in groups[bit]:
            copy.wait()
        first = pl.multiple_of((where[0] ^ bit) * rows, 128)
        left = left_ref[:, pl.ds(first, rows)]

        def step(number, carry, bit=bit, left=left):
            cols = pl.ds(pl.multiple_of(number * chunk, chunk), chunk)
            part = dot(left, held[bit, :, cols])
            out_ref[:, cols] = part if bit == 0 else out_ref[:, cols] + part
            return carry

        lax.fori_loop(0, pieces.width // chunk, step, 0)


def forward_mm(where, left, pieces, parts, after=()):
    rows, depth = left.shape
    return call(
        functools.partial(forward_body, pieces, parts),
        shape((rows, pieces.width), F32),
        [where, left, *pieces.args()],
        [
            pltpu.VMEM((parts, pieces.part_rows, pieces.width), BF),
            pltpu.SemaphoreType.DMA((pieces.copies,)),
        ],
        flops=2 * rows * depth * pieces.width,
        nbytes=2 * (rows * depth + depth * pieces.width + 2 * rows * pieces.width),
        in_specs=[SMEM, VMEM] + [HBM] * pieces.count,
        after=after,
    )


def back_body(pieces, parts, blocks, where, left_ref, *refs):
    outs, (held, sems), refs = refs[-2 - blocks : -2], refs[-2:], refs[: -2 - blocks]
    groups = fetch_parts(pieces, where, refs, held, sems, parts)
    rows = pieces.part_rows
    chunk = min(256, rows)
    tall = outs[0].shape[0]
    for bit in range(parts):
        for copy in groups[bit]:
            copy.wait()

        def step(number, carry, bit=bit):
            spot = pl.ds(pl.multiple_of(number * chunk, chunk), chunk)
            weight = held[bit, spot, :]
            first = pl.multiple_of((where[0] ^ bit) * rows + number * chunk, 128)
            for block, out_ref in enumerate(outs):
                left = left_ref[block * tall : (block + 1) * tall, :]
                out_ref[:, pl.ds(first, chunk)] = dot_cols(left, weight).astype(out_ref.dtype)
            return carry

        lax.fori_loop(0, rows // chunk, step, 0)


def back_mm(where, left, pieces, parts, kind, blocks=1, after=()):
    rows, depth = left.shape
    width = parts * pieces.part_rows
    return call(
        functools.partial(back_body, pieces, parts, blocks),
        [shape((rows // blocks, width), kind)] * blocks,
        [where, left, *pieces.args()],
        [
            pltpu.VMEM((parts, pieces.part_rows, pieces.width), BF),
            pltpu.SemaphoreType.DMA((pieces.copies,)),
        ],
        flops=2 * rows * depth * width,
        nbytes=2 * (rows * depth + depth * width + rows * width),
        in_specs=[SMEM, VMEM] + [HBM] * pieces.count,
        after=after,
    )


def spans_of(width):
    groups = [(first, min(512, width - first)) for first in range(0, width, 512)]
    return [
        (first, size, [(at_, min(256, size - at_)) for at_ in range(0, size, 256)])
        for first, size in groups
    ]


def feed_body(pieces, parts, counts, where, *refs):
    tokens, refs = refs[: counts[0]], refs[counts[0] :]
    grads, refs = refs[: counts[1]], refs[counts[1] :]
    down_ref, refs = refs[0], refs[1:]
    weights, refs = refs[: pieces.count], refs[pieces.count :]
    hid_ref, wide_ref, normed, grad, wide_w, down_w, sems = refs
    cols = pieces.width // 2
    number = 0

    def go(source, target):
        nonlocal number
        copy = pltpu.make_async_copy(source, target, sems.at[number])
        copy.start()
        number += 1
        return copy

    def stack(sources, target):
        row, copies = 0, []
        for source in sources:
            rows = source.shape[0]
            copies.append(go(source, target.at[pl.ds(row, rows), :]))
            row += rows
        return copies

    first_copies = stack(tokens, normed)
    groups = []
    for first, size, _ in spans_of(cols):
        group = []
        for bit in range(parts):
            base = pl.multiple_of((where[0] ^ bit) * pieces.part_rows, pieces.cell)
            for source, row, rows, side in pieces.moves(where, weights, bit, first, size):
                spot = pl.multiple_of(base + row, pieces.cell)
                target = wide_w.at[pl.ds(spot, rows), pl.ds(side * cols + first, size)]
                group.append(go(source, target))
        group.append(go(down_ref.at[pl.ds(first, size), :], down_w.at[pl.ds(first, size), :]))
        groups.append(group)
        if first == 0:
            first_copies += stack(grads, grad)
    for copy in first_copies:
        copy.wait()
    total = normed.shape[0]
    tall = min(512, total)
    for (first, size, pieces_), group in zip(spans_of(cols), groups):
        for copy in group:
            copy.wait()
        for offset, width in pieces_:
            left = first + offset
            gate_cols = slice(left, left + width)
            up_cols = slice(cols + left, cols + left + width)

            def step(block, carry, gate_cols=gate_cols, up_cols=up_cols):
                rows = pl.ds(pl.multiple_of(block * tall, tall), tall)
                gate = dot(normed[rows, :], wide_w[:, gate_cols])
                up = dot(normed[rows, :], wide_w[:, up_cols])
                back = dot_cols(grad[rows, :], down_w[gate_cols, :])
                sig = 1.0 / (1.0 + jnp.exp(-gate))
                silu = gate * sig
                hid_ref[rows, gate_cols] = (silu * up).astype(BF)
                wide_ref[rows, up_cols] = (back * silu).astype(BF)
                slope = sig * (1.0 + gate * (1.0 - sig))
                wide_ref[rows, gate_cols] = (back * up * slope).astype(BF)
                return carry

            lax.fori_loop(0, total // tall, step, 0)


def feed(where, tokens, grads, down, pieces, parts):
    rows = sum(a.shape[0] for a in tokens)
    depth = tokens[0].shape[1]
    cols = pieces.width // 2
    copies = len(tokens) + len(grads)
    copies += len(spans_of(cols)) * (2 * pieces.copies + 1)
    return call(
        functools.partial(feed_body, pieces, parts, (len(tokens), len(grads))),
        [
            shape((rows, cols), BF),
            shape((rows, 2 * cols), BF),
            shape((rows, depth), BF),
            shape((rows, depth), BF),
        ],
        [where, *tokens, *grads, down, *pieces.args()],
        [
            pltpu.VMEM((depth, 2 * cols), BF),
            pltpu.VMEM((cols, depth), BF),
            pltpu.SemaphoreType.DMA((copies,)),
        ],
        flops=6 * rows * depth * cols,
        nbytes=6 * depth * cols + 4 * rows * depth + 6 * rows * cols,
        in_specs=[SMEM] + [HBM] * (len(tokens) + len(grads) + 1 + pieces.count),
    )


def grad_body(more, where, left_ref, right_ref, *refs):
    total = dot_rows(left_ref[...], right_ref[...])
    if more:
        total = total.astype(BF).astype(F32) + refs[0][...].astype(F32)
    refs[-1][...] = total.astype(BF)


def grad_mm(where, left, right, side, parts, got=None, after=()):
    rows, depth = left.shape
    width = right.shape[1]
    half = depth // parts // 2
    more = got is not None
    column = lambda b, w: (0, (w[0] ^ b) * 2 + (w[2] ^ side))
    block = pl.BlockSpec((half, width), lambda b, w: (b, 0))
    return call(
        functools.partial(grad_body, more),
        shape((parts * half, width), BF),
        [where, left, right] + [got] * more,
        flops=2 * rows * parts * half * width,
        nbytes=2 * (rows * parts * half + rows * width + parts * half * width),
        grid=(parts,),
        in_specs=[
            pl.BlockSpec((rows, half), column),
            pl.BlockSpec((rows, width), lambda b, w: (0, 0)),
        ]
        + [block] * more,
        out_specs=block,
        after=after,
        prefetch=True,
    )


def grad_columns(where, left, right, side, got=None, after=()):
    rows, depth = left.shape
    width = right.shape[1] // 2
    steps = 2
    more = got is not None
    column = lambda n, w: (0, (w[2] ^ side) * steps + n)
    block = pl.BlockSpec((depth, width // steps), lambda n, w: (0, n))
    return call(
        functools.partial(grad_body, more),
        shape((depth, width), BF),
        [where, left, right] + [got] * more,
        flops=2 * rows * depth * width,
        nbytes=2 * (rows * depth + rows * width + depth * width),
        grid=(steps,),
        in_specs=[
            pl.BlockSpec((rows, depth), lambda n, w: (0, 0)),
            pl.BlockSpec((rows, width // steps), column),
        ]
        + [block] * more,
        out_specs=block,
        after=after,
        prefetch=True,
    )


def mix_body(left_ref, right_ref, out_ref):
    out_ref[...] = dot(left_ref[...], right_ref[...]).astype(BF)


def mix(left, right, blocks, after=()):
    rows, depth = left.shape
    width = right.shape[1]
    return call(
        mix_body,
        shape((rows, width), BF),
        [left, right],
        flops=2 * rows * depth * width,
        nbytes=2 * (rows * depth + depth * width + rows * width),
        grid=(blocks,),
        in_specs=[
            pl.BlockSpec((rows // blocks, depth), lambda n: (n, 0)),
            pl.BlockSpec((depth, width), lambda n: (0, 0)),
        ],
        out_specs=pl.BlockSpec((rows // blocks, width), lambda n: (n, 0)),
        after=after,
    )


def key_value_body(pieces, parts, where, x_ref, gain_ref, cos_ref, sin_ref, tag_ref, *refs):
    (normed_ref, out_ref, held, sems), refs = refs[-4:], refs[:-4]
    groups = fetch_parts(pieces, where, refs, held, sems, parts)
    x = x_ref[...].astype(F32)
    normed_ref[...] = (x * rms_scale(x) * gain_ref[0:1, :]).astype(BF)
    rows = x.shape[0]
    both = 0.0
    for bit in range(parts):
        for copy in groups[bit]:
            copy.wait()
        first = pl.multiple_of((where[0] ^ bit) * pieces.part_rows, 128)
        both = both + dot(normed_ref[:, pl.ds(first, pieces.part_rows)], held[bit])
    cosine = jnp.concatenate([cos_ref[...]] * (KW // 128), 1)
    sine = jnp.concatenate([sin_ref[...]] * (KW // 128), 1)
    keys = spin(both[:, :KW], cosine, sine)
    out_ref[:rows, :KW] = keys.astype(BF)
    out_ref[:rows, KW:] = both[:, KW:].astype(BF)
    out_ref[rows:, :] = tag_ref[...]


def seq_keys(kv_refs, seq, head, tok):
    rows = pl.ds(seq * tok, tok)
    found = []
    for first in (head * HD, KW + head * HD):
        sides = [ref[:, rows, first : first + HD].reshape(-1, HD) for ref in kv_refs]
        found.append(jnp.concatenate(sides, 0))
    return found


def fill_bias(kv_refs, tag_ref, bias_ref, seq, tok, rows):
    levels = kv_refs[0].shape[0]
    row = lax.broadcasted_iota(jnp.int32, (EXTRA, 128), 0)

    def start_of(block):
        return jnp.sum(jnp.where(row == seq, block.astype(F32), 0.0), 0, keepdims=True)

    own = start_of(tag_ref[:, 0:128])
    ahead = (
        lax.broadcasted_iota(jnp.int32, (tok, 128), 0)
        - lax.broadcasted_iota(jnp.int32, (tok, 128), 1)
    ).astype(F32)
    for run in range(2 * levels):
        tags = kv_refs[run // levels][run % levels, rows : rows + EXTRA, 0:128]
        lead = (start_of(tags) - own) * float(tok)
        block = jnp.where(ahead + lead <= 0.0, 0.0, MASKED)
        bias_ref[run * tok : (run + 1) * tok, :] = jnp.concatenate([block, block], 1)


def stack_heads(two):
    return jnp.concatenate([two[:, :HD], two[:, HD:]], 0)


def lay_heads(stacked):
    tok = stacked.shape[0] // 2
    return jnp.concatenate([stacked[:tok], stacked[tok:]], 1)


def attend_body(seq, q_ref, kept_ref, other_ref, tag_ref, cos_ref, sin_ref, rot_ref, out_ref, log_ref, bias_ref):
    tok = q_ref.shape[0]
    kv_refs = (kept_ref, other_ref)
    rows = kept_ref.shape[1] - EXTRA
    fill_bias(kv_refs, tag_ref, bias_ref, seq, tok, rows)
    for head in range(KVH):
        keys, values = seq_keys(kv_refs, seq, head, tok)
        values_t = values.astype(F32).T.astype(BF)

        def pair(number, carry, head=head, keys=keys, values_t=values_t):
            first = head * GROUP + 2 * number
            lanes = pl.ds(pl.multiple_of(first * HD, 128), 128)
            turned = spin(q_ref[:, lanes], cos_ref[...], sin_ref[...]).astype(BF)
            turned = turned * jnp.asarray(HD**-0.5, BF)
            rot_ref[:, lanes] = turned
            scores = dot_cols(keys, stack_heads(turned)) + bias_ref[...]
            top = jnp.max(scores, 0, keepdims=True)
            weights = jnp.exp(scores - top)
            total = jnp.sum(weights, 0, keepdims=True)
            shares = (weights * (1.0 / total)).astype(BF)
            mixed = dot(values_t, shares).T
            out_ref[:, lanes] = lay_heads(mixed).astype(BF)
            logs = top + jnp.log(total)
            log_ref[0, pl.ds(first, 1), :] = logs[:, :tok]
            log_ref[0, pl.ds(first + 1, 1), :] = logs[:, tok:]
            return carry

        lax.fori_loop(0, GROUP // 2, pair, 0)


def attend(seq, query_raw, kv, tag, cosine, sine, tok, after=()):
    width = query_raw.shape[1]
    runs = 2 * kv[0].shape[0]
    block = pl.BlockSpec((tok, width), lambda s: (seq, 0))
    table = pl.BlockSpec((tok, 128), lambda s: (seq, 0))
    fixed = lambda dims: pl.BlockSpec(dims, lambda s: (0,) * len(dims))
    return call(
        functools.partial(attend_body, seq),
        [shape((tok, width), BF), shape((tok, width), BF), shape((1, H, tok), F32)],
        [query_raw, *kv, tag, cosine, sine],
        [pltpu.VMEM((runs * tok, 2 * tok), F32)],
        flops=16 * H * tok * runs * tok * HD,
        nbytes=tok * width * 8,
        grid=(1,),
        in_specs=[block, fixed(kv[0].shape), fixed(kv[0].shape), fixed(tag.shape), table, table],
        out_specs=[fixed((tok, width)), fixed((tok, width)), fixed((1, H, tok))],
        after=after,
    )


def attend_back_body(
    seq, heads, rot_ref, kept_ref, other_ref, tag_ref, log_ref, grad_ref, cos_ref, sin_ref, dq_ref,
    dkept_ref, dother_ref, bias_ref, dk_ref, dv_ref,
):
    tok = rot_ref.shape[0]
    kv_refs = (kept_ref, other_ref)
    rows = kept_ref.shape[1] - EXTRA
    levels = kept_ref.shape[0]
    fill_bias(kv_refs, tag_ref, bias_ref, seq, tok, rows)
    for head in heads:
        keys, values = seq_keys(kv_refs, seq, head, tok)
        keys_t = keys.astype(F32).T.astype(BF)
        dk_ref[...] = jnp.zeros_like(dk_ref)
        dv_ref[...] = jnp.zeros_like(dv_ref)

        def pair(number, carry, head=head, keys=keys, values=values, keys_t=keys_t):
            first = head * GROUP + 2 * number
            lanes = pl.ds(pl.multiple_of((first - heads[0] * GROUP) * HD, 128), 128)
            queries = stack_heads(rot_ref[:, lanes])
            grads = stack_heads(grad_ref[:, lanes])
            logs = jnp.concatenate(
                [log_ref[0, pl.ds(first, 1), :], log_ref[0, pl.ds(first + 1, 1), :]], 1
            )
            shares = jnp.exp(dot_cols(keys, queries) + bias_ref[...] - logs)
            grad_shares = dot_cols(values, grads)
            inner = jnp.sum(shares * grad_shares, 0, keepdims=True)
            grad_scores = (shares * (grad_shares - inner)).astype(BF)
            dk_ref[...] += dot(grad_scores, queries)
            dv_ref[...] += dot(shares.astype(BF), grads)
            grad_q = (dot(keys_t, grad_scores) * HD**-0.5).T
            grad_q = spin(lay_heads(grad_q), cos_ref[...], -sin_ref[...])
            dq_ref[:, lanes] = grad_q.astype(BF)
            return carry

        lax.fori_loop(0, GROUP // 2, pair, 0)
        low, high = (head - heads[0]) * HD, (head - heads[0] + 1) * HD
        step = len(heads) * HD
        for side, out_ref in enumerate((dkept_ref, dother_ref)):
            span = slice(side * levels * tok, (side + 1) * levels * tok)
            out_ref[:, :, low:high] = dk_ref[span, :].astype(BF).reshape(levels, tok, HD)
            out_ref[:, :, step + low : step + high] = (
                dv_ref[span, :].astype(BF).reshape(levels, tok, HD)
            )


def attend_back(seq, heads, rot, kv, tag, logs, grad, cosine, sine, tok, after=()):
    width = len(heads) * GROUP * HD
    lane = heads[0] // len(heads)
    runs = 2 * kv[0].shape[0]
    table = pl.BlockSpec((tok, 128), lambda s: (seq, 0))
    fixed = lambda dims: pl.BlockSpec(dims, lambda s: (0,) * len(dims))
    moved = (runs // 2, tok, 2 * len(heads) * HD)
    return call(
        functools.partial(attend_back_body, seq, heads),
        [shape((tok, width), BF)] + [shape(moved, BF)] * 2,
        [rot, *kv, tag, logs, grad, cosine, sine],
        [
            pltpu.VMEM((runs * tok, 2 * tok), F32),
            pltpu.VMEM((runs * tok, HD), F32),
            pltpu.VMEM((runs * tok, HD), F32),
        ],
        flops=10 * len(heads) * GROUP * tok * runs * tok * HD,
        nbytes=tok * width * 8,
        grid=(1,),
        in_specs=[
            pl.BlockSpec((tok, width), lambda s: (0, lane)),
            fixed(kv[0].shape),
            fixed(kv[0].shape),
            fixed(tag.shape),
            fixed((1, H, tok)),
            pl.BlockSpec((tok, width), lambda s: (seq, lane)),
            table,
            table,
        ],
        out_specs=[fixed((tok, width))] + [fixed(moved)] * 2,
        after=after,
    )


def kv_back_body(*refs):
    parts, (cos_ref, sin_ref, out_ref) = refs[:-3], refs[-3:]
    total = parts[0][...].astype(F32)
    for part in parts[1:]:
        total = total + part[...].astype(F32)
    cosine = jnp.concatenate([cos_ref[...]] * (KW // 128), 1)
    sine = jnp.concatenate([sin_ref[...]] * (KW // 128), 1)
    out_ref[:, :KW] = spin(total[:, :KW], cosine, -sine).astype(BF)
    out_ref[:, KW:] = total[:, KW:].astype(BF)


def place_body(plan, count, outs, where, *refs):
    pieces, targets = refs[:count], refs[count : count + outs]
    held, wide, in_sems, out_sems = refs[count + outs :]
    mine, core = where[0], where[2]
    reads, writes = [], []
    for number, (piece, first, column, rows, cols, target, place) in enumerate(plan):
        slot = number % 2
        top, left = place(mine, core)
        reads.append(
            pltpu.make_async_copy(
                pieces[piece].at[pl.ds(first, rows), pl.ds(column, cols)],
                held.at[slot, pl.ds(0, rows), pl.ds(0, cols)],
                in_sems.at[slot],
            )
        )
        writes.append(
            pltpu.make_async_copy(
                wide.at[slot, pl.ds(0, rows), pl.ds(0, cols)],
                targets[target].at[pl.ds(top, rows), pl.ds(left, cols)],
                out_sems.at[slot],
            )
        )
    reads[0].start()
    for number, (_, _, _, rows, cols, _, _) in enumerate(plan):
        slot = number % 2
        if number + 1 < len(plan):
            reads[number + 1].start()
        reads[number].wait()
        if number >= 2:
            writes[number - 2].wait()
        wide[slot, :rows, :cols] = held[slot, :rows, :cols].astype(F32)
        writes[number].start()
    for copy in writes[-2:]:
        copy.wait()


def place(where, pieces, plan, outs):
    hbm = pl.BlockSpec(memory_space=pl.ANY)
    rows = max(step[3] for step in plan)
    cols = max(step[4] for step in plan)
    moved = sum(step[3] * step[4] for step in plan)
    return call(
        functools.partial(place_body, plan, len(pieces), len(outs)),
        [shape(dims, F32) for dims in outs],
        [where, *pieces],
        [
            pltpu.VMEM((2, rows, cols), BF),
            pltpu.VMEM((2, rows, cols), F32),
            pltpu.SemaphoreType.DMA((2,)),
            pltpu.SemaphoreType.DMA((2,)),
        ],
        nbytes=6 * moved,
        in_specs=[pl.BlockSpec(memory_space=pltpu.SMEM)] + [hbm] * len(pieces),
        out_specs=[hbm] * len(outs),
    )


def on_device(
    hidden_in,
    positions,
    cotangent,
    norm_gain,
    w_query,
    w_key,
    w_value,
    w_out,
    ffn_gain,
    w_gate,
    w_up,
    w_down,
):
    seq_count, tok_count, model_width = hidden_in.shape
    row_count = seq_count * tok_count
    parts = lax.axis_size("fsdp")
    runs = lax.axis_size("ctx")
    levels = runs // 2
    mine = lax.axis_index("fsdp").astype(jnp.int32)
    run = lax.axis_index("ctx").astype(jnp.int32)
    core = lax.rem(run, 2)
    level = run // 2
    quarter = lax.rem(run, 4)
    where = jnp.stack([mine, quarter, core, level])
    shard = model_width // parts
    half = shard // 2
    ff_part = w_down.shape[0]
    aligned = ff_part % 128 == 0

    def hop(array, bit):
        return lax.ppermute(array, "fsdp", [(i, i ^ bit) for i in range(parts)])

    def swap_run(array, bit):
        return lax.ppermute(array, "ctx", [(i, i ^ bit) for i in range(runs)])

    def level_send(array, pairs):
        return lax.ppermute(
            array, "ctx", [(2 * a + k, 2 * b + k) for a, b in pairs for k in range(2)]
        )

    def tie(values, *after):
        many = isinstance(values, (list, tuple))
        flat = list(values) if many else [values]
        tied = lax.optimization_barrier((*flat, *after))[: len(flat)]
        return list(tied) if many else tied[0]

    def add(a, b):
        return (a.astype(F32) + b.astype(F32)).astype(BF)

    def spread(local):
        if parts != 4:
            return [hop(local, bit) for bit in range(1, parts)]
        middle = local.shape[0] // 2
        from_x, from_y = hop(local, 1), hop(local, 2)
        return [from_x, from_y, hop(from_x[:middle], 2), hop(from_y[middle:], 1)]

    def halves(own, pieces, others, width):
        cell = own[0].shape[0] // 2
        blocks = [(bit - 1, 0, 0, 0, bit) for bit in range(1, parts)]
        bit = 1
        for number, other in enumerate(others):
            for row in range(0, other.shape[0], cell):
                blocks.append((parts - 1 + number, row, 0, 1, bit))
                bit += 1
        return Pieces(own, pieces + list(others), blocks, cell, width)

    def hops(local):
        return [hop(local, bit) for bit in range(1, parts)]

    def turn(array):
        return level_send(array, [(i, (i + 1) % levels) for i in range(levels)])

    def columns_of(sources, index, cols):
        cell = sources[0].shape[0] // runs
        return jnp.concatenate(
            [lax.dynamic_slice(a, (run * cell, index * cols), (cell, cols)) for a in sources],
            1,
        )

    def lay_rows(pieces):
        rows, cell, width = pieces.part_rows, pieces.cell, pieces.width
        step = width // len(pieces.own)
        local = jnp.concatenate([at(a, mine * step, step, 1) for a in pieces.own], 1)
        whole = jnp.zeros((parts * rows, width), BF)
        whole = lax.dynamic_update_slice(whole, local, (mine * rows, 0))
        for source, first, back, flip, bit in pieces.blocks:
            side = lax.rem(level + levels - back, levels) * 2 + (core ^ flip)
            spot = (mine ^ bit) * rows + side * cell
            piece = pieces.sources[source][first : first + cell]
            whole = lax.dynamic_update_slice(whole, piece, (spot, 0))
        return whole

    def sum_first(blocks):
        if parts != 4:
            return [hop(blocks[bit], bit) for bit in range(1, parts)]
        middle = blocks[0].shape[0] // 2
        return [hop(blocks[3][middle:], 1), hop(blocks[3][:middle], 2)]

    def sum_second(blocks, got):
        if parts != 4:
            return got
        middle = blocks[0].shape[0] // 2
        to_x = jnp.concatenate([add(blocks[1][:middle], got[1]), blocks[1][middle:]], 0)
        to_y = jnp.concatenate([blocks[2][:middle], add(blocks[2][middle:], got[0])], 0)
        return [hop(to_x, 1), hop(to_y, 2)]

    def sum_last(blocks, got):
        return sum([a.astype(F32) for a in got], blocks[0].astype(F32))

    def far_of(pieces):
        if parts != 4:
            return []
        half_ = pieces[0].shape[0] // 2
        return [hop(pieces[0][:half_], 2), hop(pieces[1][half_:], 1)]

    def near_of(local):
        return [hop(local, bit) for bit in ((1, 2) if parts == 4 else range(1, parts))]

    middle_level = levels // 2
    last_level = levels - 1
    ups = [[(s, s + 1), (last_level - s, last_level - s - 1)] for s in range(middle_level - 1)]
    over = [(middle_level - 1, middle_level), (middle_level, middle_level - 1)]
    downs = [[(b, a) for a, b in pairs] for pairs in reversed(ups)]

    class Climb:
        def __init__(self, value):
            self.value, self.stage = value, 0

        def start(self):
            self.moving = level_send(self.value, (ups + [over] + downs)[self.stage])
            return self.moving

        def take(self, got):
            if self.stage < middle_level:
                self.value = add(self.value, got)
            else:
                s = 2 * middle_level - 2 - self.stage
                ends = (level == s) | (level == last_level - s)
                self.value = jnp.where(ends, got, self.value)
            self.stage += 1

        @property
        def done(self):
            return self.stage == 2 * middle_level - 1

    def complete(climb):
        while not climb.done:
            climb.take(climb.start())
        return climb

    def both_ways(new, old):
        if levels != 4 or new.value.shape != old.value.shape:
            return [new.start(), old.start()]
        inner = (level == 1) | (level == 2)
        sent = jnp.where(inner, old.value, new.value)
        return [level_send(sent, [(0, 1), (1, 0), (2, 3), (3, 2)])]

    def take_both(new, old, got):
        if len(got) == 2:
            new.take(got[0])
            old.take(got[1])
            return
        inner = (level == 1) | (level == 2)
        new.value = jnp.where(inner, add(new.value, got[0]), new.value)
        old.value = jnp.where(inner, old.value, got[0])
        new.stage += 1
        old.stage += 1

    def advance(climbs):
        return [c.start() for c in climbs]

    def take(climbs, results):
        for climb, got in zip(climbs, results):
            climb.take(got)

    gains = jnp.stack([norm_gain, ffn_gain] + [jnp.zeros_like(norm_gain)] * (EXTRA - 2), 0)
    own_kv = jnp.concatenate([w_key, w_value], 1)
    wide = own_kv.shape[1] // shard
    tag_rows = jnp.concatenate([gains] * wide, 1)
    sent_kv = jnp.concatenate([at(own_kv, core * half, half), tag_rows], 0)
    got_kv = [hop(sent_kv, bit) for bit in range(1, parts)]
    own_query = at(w_query, core * half, half)
    near_query = [hop(own_query, bit) for bit in range(1, min(3, parts))]
    got_kv = tie(got_kv)
    kv_pieces = [a[:half] for a in got_kv]
    other_kv = swap_run(jnp.concatenate(kv_pieces, 0), 1)
    rest_query = [hop(tie(own_query, *got_kv), bit) for bit in range(3, parts)]
    key_value_w = halves([own_kv], kv_pieces, [other_kv], own_kv.shape[1])
    gain_cells = [gains] + [a[half:, :shard] for a in got_kv]
    all_gains = jnp.zeros((EXTRA, model_width), BF)
    for bit in range(parts):
        all_gains = lax.dynamic_update_slice(
            all_gains, gain_cells[bit], (0, (mine ^ bit) * shard)
        )
    all_gains = all_gains.astype(F32)
    gain_one, gain_two = all_gains[0], all_gains[1]

    spread_of = 10000.0 ** (-jnp.arange(HD // 2, dtype=F32) / (HD // 2))
    turned = positions.astype(F32).reshape(row_count, 1) * spread_of
    cosine = jnp.concatenate([jnp.cos(turned)] * 4, 1)
    sine = jnp.concatenate([-jnp.sin(turned), jnp.sin(turned)] * 2, 1)
    starts = (positions[:, :1] // tok_count).astype(BF)
    tag = jnp.concatenate(
        [
            jnp.broadcast_to(starts, (seq_count, 2 * KW)),
            jnp.zeros((EXTRA - seq_count, 2 * KW), BF),
        ],
        0,
    )

    x_low = hidden_in.reshape(row_count, model_width)
    normed_one, packed = call(
        functools.partial(key_value_body, key_value_w, parts),
        [shape((row_count, model_width), BF), shape((row_count + EXTRA, 2 * KW), BF)],
        [where, x_low, all_gains, cosine, sine, tag, *key_value_w.args()],
        [
            pltpu.VMEM((parts, shard, 2 * KW), BF),
            pltpu.SemaphoreType.DMA((key_value_w.copies,)),
        ],
        flops=4 * row_count * model_width * KW,
        nbytes=row_count * model_width * 4 + model_width * KW * 4,
        in_specs=[SMEM] + [VMEM] * 5 + [HBM] * key_value_w.count,
    )
    turns = [packed]
    while len(turns) < levels:
        turns.append(turn(turns[-1]))
    got_query = tie(near_query + rest_query, turns[-1])
    kept_kv = jnp.stack(turns, 0)
    kv = [kept_kv, swap_run(kept_kv, 1)]
    other_query = swap_run(jnp.concatenate(got_query, 0), 1)
    sent_wide = [columns_of([w_gate, w_up], mine ^ bit, ff_part) for bit in range(1, parts)]
    sent_wide = tie(sent_wide, *got_query)
    wide_hops = [hop(a, bit + 1) for bit, a in enumerate(sent_wide)]
    query_w = halves([w_query], got_query, [other_query], w_query.shape[1])
    query_raw = forward_mm(where, normed_one, query_w, parts)

    wide_hops = tie(wide_hops, query_raw)
    rings = [jnp.concatenate(wide_hops, 0)]
    moving = turn(rings[0])
    near_out = near_of(at(tie(w_out, *wide_hops), core * half, half))
    forward = [
        attend(0, query_raw, kv, tag, cosine, sine, tok_count, after=[rings[0]])
    ]
    moving, *near_out = tie([moving, *near_out], forward[0][1])
    rings.append(moving)
    moving = turn(rings[1])
    far_out = far_of(near_out)
    grad_y_low = cotangent.reshape(row_count, model_width)
    near_dm = near_of(tie(grad_y_low, *near_out))
    for seq in range(1, seq_count):
        forward.append(
            attend(
                seq, query_raw, kv, tag, cosine, sine, tok_count, after=[rings[-1], *near_out]
            )
        )
    rot, attended, logs = [list(a) for a in zip(*forward)]
    moving, *far_out = tie([moving, *far_out], attended[-1])
    rings.append(moving)
    far_out = [jnp.concatenate(far_out, 0)] if parts == 4 else far_out
    got_out = near_out + far_out
    other_out = [swap_run(jnp.concatenate(got_out, 0), 1)]
    while len(rings) < levels - 1:
        rings.append(turn(rings[-1]))
    moving = turn(rings[-1])
    out_w = halves([w_out], got_out, other_out, w_out.shape[1])
    attended = jnp.concatenate(attended, 0)
    inputs = x_low.astype(F32)
    residual = inputs + forward_mm(where, attended, out_w, parts)
    scale_two = rms_scale(residual)
    normed_two = (residual * scale_two * gain_two).astype(BF)
    near_normed = near_of(normed_two)
    far_dm = far_of(tie(near_dm, residual))
    far_normed = far_of(near_normed)
    rings.append(moving)
    other_wide = swap_run(jnp.concatenate(rings, 0), 1)
    all_normed = [normed_two] + near_normed + far_normed
    all_dm = [grad_y_low] + near_dm + far_dm
    cell = shard // runs
    blocks = []
    for back in range(levels):
        for bit in range(1, parts):
            blocks.append((back, (bit - 1) * cell, back, 0, bit))
            blocks.append((levels, (back * (parts - 1) + bit - 1) * cell, back, 1, bit))
    wide_w = Pieces([w_gate, w_up], rings + [other_wide], blocks, cell, 2 * ff_part, levels)

    if aligned:
        hidden_low, grad_wide_in, stacked, stacked_dm = feed(
            where, all_normed, all_dm, w_down, wide_w, parts
        )
    else:
        laid = lay_rows(wide_w)
        stacked, stacked_dm = jnp.concatenate(all_normed, 0), jnp.concatenate(all_dm, 0)
        gate_proj, up_proj = dot(stacked, laid[:, :ff_part]), dot(stacked, laid[:, ff_part:])
        sigmoid_gate = jax.nn.sigmoid(gate_proj)
        hidden_low = (gate_proj * sigmoid_gate * up_proj).astype(BF)
        grad_hidden = dot_cols(stacked_dm, w_down)
        grad_up_in = (grad_hidden * gate_proj * sigmoid_gate).astype(BF)
        slope = sigmoid_gate * (1.0 + gate_proj * (1.0 - sigmoid_gate))
        grad_wide_in = jnp.concatenate(
            [(grad_hidden * up_proj * slope).astype(BF), grad_up_in], 1
        )

    def blocks_of(total):
        return [total[b * half : (b + 1) * half] for b in range(parts)]

    def split(both, *counts):
        out = []
        for count in counts:
            out.append(both[:count])
            both = both[count:]
        return [*out, both]

    def values(climbs):
        return [c.value for c in climbs]

    down_rows = ff_part // 2
    middle = model_width // 2

    def both_rows(done, first, cols, target, row=0):
        return [
            (done[0], first, cols, target, lambda m, k: (k * half + row, 0)),
            (done[1], first, cols, target, lambda m, k: ((1 - k) * half + row, 0)),
        ]

    def put(steps, outs):
        pieces, plan = [], []
        for piece, column, cols, target, spot in steps:
            if not any(piece is p for p in pieces):
                pieces.append(piece)
            index = [piece is p for p in pieces].index(True)
            rows = piece.shape[0]
            plan.append((index, 0, column, rows, cols, target, spot))
        return place(where, pieces, plan, outs)

    full = (shard, parts * ff_part)

    def place_wide(wide_done):
        if not aligned:
            outs = [jnp.zeros(full, F32), jnp.zeros(full, F32)]
            for bit in range(parts):
                for side in range(2):
                    spot = ((core ^ side) * half, (mine ^ bit) * ff_part)
                    piece = wide_done[bit][side].astype(F32)
                    for number in range(2):
                        part = piece[:, number * ff_part : (number + 1) * ff_part]
                        outs[number] = lax.dynamic_update_slice(outs[number], part, spot)
            return outs
        steps = []
        for bit in range(parts):
            for side in range(2):
                for target in range(2):

                    def spot(m, k, bit=bit, side=side):
                        row = pl.multiple_of((k ^ side) * half, half)
                        return row, pl.multiple_of((m ^ bit) * ff_part, 128)

                    steps.append(
                        (wide_done[bit][side], target * ff_part, ff_part, target, spot)
                    )
        return put(steps, [full, full])

    def place_down(down_done):
        if not aligned:
            out = jnp.zeros((ff_part, model_width), F32)
            for number in range(2):
                for side in range(2):
                    spot = (number * down_rows, (core ^ side) * middle)
                    piece = down_done[number][side].astype(F32)
                    out = lax.dynamic_update_slice(out, piece, spot)
            return out
        steps = []
        for number in range(2):
            for side in range(2):

                def spot(m, k, number=number, side=side):
                    return number * down_rows, pl.multiple_of((k ^ side) * middle, 128)

                steps.append((down_done[number][side], 0, middle, 0, spot))
        return put(steps, [(ff_part, model_width)])[0]

    def sync(*groups):
        flat = [a for group in groups for a in group]
        flat = list(lax.optimization_barrier(tuple(flat)))
        out = []
        for group in groups:
            out.append(flat[: len(group)])
            flat = flat[len(group) :]
        return out

    def sync_climbs(climbs, *groups):
        held, *rest = sync(values(climbs), *groups)
        for climb, value in zip(climbs, held):
            climb.value = value
        return rest

    down_sent = dot_rows(hidden_low, at(stacked_dm, (1 - core) * middle, middle, 1)).astype(BF)
    (down_sent,), (hidden_low,) = sync([down_sent], [hidden_low])
    down_got = swap_run(down_sent, 1)
    down_kept = dot_rows(hidden_low, at(stacked_dm, core * middle, middle, 1)).astype(BF)
    down_pair = add(down_kept, down_got)
    down = [Climb(down_pair[i * down_rows : (i + 1) * down_rows]) for i in range(2)]

    moving = advance(down[:1])
    if aligned:
        back_blocks = back_mm(
            where, grad_wide_in, wide_w, parts, BF, parts, after=values(down)
        )
    else:
        back_rows = dot_cols(grad_wide_in, laid).astype(BF)
        back_blocks = [back_rows[i * row_count : (i + 1) * row_count] for i in range(parts)]
    back_got = sum_first(back_blocks)
    wide_sent = grad_mm(where, stacked, grad_wide_in, 1, parts, after=back_blocks[:1])
    take(down[:1], moving)
    (wide_sent,), back_got = sync_climbs(down, [wide_sent], back_got)

    moving = advance(down)
    wide_got = swap_run(wide_sent, 1)
    back_got = sum_second(back_blocks, back_got)
    mixed = mix(hidden_low, w_down, parts, after=[wide_sent, *values(down)])
    wide_pair = grad_mm(
        where, stacked, grad_wide_in, 0, parts, got=wide_got, after=[mixed]
    )
    take(down, moving)
    (wide_pair,), back_got, (mixed,) = sync_climbs(down, [wide_pair], back_got, [mixed])
    wide_blocks = blocks_of(wide_pair)
    mixed_blocks = [mixed[i * row_count : (i + 1) * row_count] for i in range(parts)]

    climbs = [Climb(wide_blocks[0])]
    moving = advance(down + climbs)
    near_wide = [hop(a, bit + 1) for bit, a in enumerate(wide_blocks[1:3])]
    grad_normed_two = sum_last(back_blocks, back_got)
    grad_y = grad_y_low.astype(F32)
    grad_res_norm, grad_gain_two = norm_back(grad_normed_two, residual, scale_two, gain_two)
    grad_residual = grad_y + grad_res_norm
    grad_proj = grad_residual.astype(BF)
    (grad_attended,) = back_mm(where, grad_proj, out_w, parts, BF, after=values(down))
    backward = []

    def pull(seq, number, after=()):
        heads = range(number * KVH // 2, (number + 1) * KVH // 2)
        after = list(after) + [a[0] for a in backward[-1:]]
        backward.append(
            attend_back(
                seq, heads, rot[seq], kv, tag, logs[seq], grad_attended, cosine, sine,
                tok_count, after=after,
            )
        )

    def sync_pulled(climbs, *groups):
        pulled, *rest = sync_climbs(climbs, backward[-1], *groups)
        backward[-1] = pulled
        return rest

    pull(0, 0, values(down))
    take(down + climbs, moving)
    (near_wide,) = sync_pulled(down + climbs, near_wide)

    climbs += [Climb(a) for a in near_wide]
    moving = advance(down[1:] + climbs[:2])
    rest_wide = [hop(wide_blocks[b], b) for b in range(3, parts)]
    pull(0, 1, values(down + climbs))
    pull(1, 0)
    take(down[1:] + climbs[:2], moving)
    (rest_wide,) = sync_pulled(down + climbs, rest_wide)

    climbs += [Climb(a) for a in rest_wide]
    moving = advance(climbs[1:2])
    merged = both_ways(climbs[2], climbs[0])
    swap_down = [swap_run(complete(c).value, 1) for c in down]
    pull(1, 1, values(climbs))
    for seq in range(2, seq_count):
        for number in range(2):
            pull(seq, number)

    def lay(index):
        rows = [
            [backward[2 * seq + number][index] for number in range(2)]
            for seq in range(seq_count)
        ]
        if index == 0:
            return jnp.concatenate([jnp.concatenate(r, 1) for r in rows], 0)
        step = KW // 2
        keys = jnp.concatenate([jnp.concatenate([a[..., :step] for a in r], 2) for r in rows], 1)
        rest = jnp.concatenate([jnp.concatenate([a[..., step:] for a in r], 2) for r in rows], 1)
        return jnp.concatenate([keys, rest], 2)

    out_sent = grad_mm(where, attended, grad_proj, 1, parts, after=[backward[-1][0]])
    grad_query_low = lay(0)
    query_sent = grad_mm(where, normed_one, grad_query_low, 1, parts, after=[out_sent])
    take(climbs[1:2], moving)
    take_both(climbs[2], climbs[0], merged)
    (out_sent, query_sent), swap_down = sync_pulled(
        climbs, [out_sent, query_sent], swap_down
    )

    moving = advance(climbs[2:3])
    merged = both_ways(climbs[3], climbs[1])
    other_dkv = swap_run(lay(2), 1)
    out_got = swap_run(out_sent, 1)
    by_level = add(lay(1), other_dkv)
    ring_kv = by_level[levels - 1]
    for step in reversed(range(1, levels)):
        ring_kv = level_send(ring_kv, [(i, (i - 1) % levels) for i in range(levels)])
        if step > 1:
            ring_kv = add(ring_kv, by_level[step - 1])
    out_pair = grad_mm(
        where, attended, grad_proj, 0, parts, got=out_got, after=[by_level, *values(climbs)]
    )
    (out_pair,), (query_sent,) = sync([out_pair], [query_sent])
    query_got = swap_run(query_sent, 1)
    (grad_normed_one,) = back_mm(where, grad_query_low, query_w, parts, F32, after=[out_pair])
    query_pair = grad_mm(
        where, normed_one, grad_query_low, 0, parts, got=query_got, after=[grad_normed_one]
    )
    take(climbs[2:3], moving)
    take_both(climbs[3], climbs[1], merged)
    (ring_kv,), (out_pair, query_pair) = sync_climbs(climbs, [ring_kv], [out_pair, query_pair])
    out_blocks, query_blocks = blocks_of(out_pair), blocks_of(query_pair)

    moving = advance(climbs[2:])
    out_got = sum_first(out_blocks)
    grad_kv_low = call(
        kv_back_body,
        shape((row_count, 2 * KW), BF),
        [by_level[0], ring_kv, cosine, sine],
        nbytes=row_count * KW * 4 * (levels + 1),
        after=values(climbs),
    )
    kv_sent = grad_mm(where, normed_one, grad_kv_low, 1, parts)
    out_got, (kv_sent,) = sync(out_got, [kv_sent])
    out_got = sum_second(out_blocks, out_got)
    kv_got = swap_run(kv_sent, 1)
    (grad_normed_kv,) = back_mm(where, grad_kv_low, key_value_w, parts, F32, after=[kv_sent])
    kv_pair = grad_mm(
        where, normed_one, grad_kv_low, 0, parts, got=kv_got, after=[grad_normed_kv]
    )
    grad_normed_one = grad_normed_one + grad_normed_kv
    scale_one = rms_scale(inputs)
    grad_in_norm, grad_gain_one = norm_back(grad_normed_one, inputs, scale_one, gain_one)
    grad_in = (grad_residual + grad_in_norm).reshape(seq_count, tok_count, model_width)
    gain_rows = jnp.stack([grad_gain_one, grad_gain_two], 0).astype(BF)
    gain_rows = gain_rows.reshape(2, parts, 2, half)
    gain_rows = jnp.concatenate(
        [lax.dynamic_slice(gain_rows, (0, mine ^ b, 0, 0), (2, 1, 2, half)) for b in range(parts)],
        1,
    )
    gain_sent = at(gain_rows, 1 - core, 1, 2).reshape(2, parts * half)
    gain_kept = at(gain_rows, core, 1, 2).reshape(2, parts * half)
    gain_cols = add(gain_kept, swap_run(gain_sent, 1)).T
    gain_cols = jnp.concatenate([gain_cols, jnp.zeros((parts * half, 126), BF)], 1)
    kv_blocks = blocks_of(jnp.concatenate([kv_pair, gain_cols], 1))
    take(climbs[2:], moving)
    out_got, kv_blocks, (grad_in,) = sync_climbs(climbs, out_got, kv_blocks, [grad_in])

    out_climb = Climb(sum_last(out_blocks, out_got).astype(BF))
    moving = advance([climbs[3], out_climb])
    query_mid = sum_first(query_blocks)
    swap_wide = [swap_run(complete(c).value, 1) for c in climbs[:2]]
    query_mid, swap_wide = sync(query_mid, swap_wide)
    query_end = sum_second(query_blocks, query_mid)
    kv_mid = sum_first(kv_blocks)
    take([climbs[3], out_climb], moving)
    query_end, kv_mid = sync_climbs([climbs[3], out_climb], query_end, kv_mid)

    query_climb = Climb(sum_last(query_blocks, query_end).astype(BF))
    moving = advance([out_climb, query_climb])
    kv_end = sum_second(kv_blocks, kv_mid)
    swap_wide += [swap_run(complete(c).value, 1) for c in climbs[2:]]
    down_done = [[c.value, s] for c, s in zip(down, swap_down)]
    grad_down = place_down(down_done)
    take([out_climb, query_climb], moving)
    kv_end, swap_wide, (grad_down,) = sync_climbs(
        [out_climb, query_climb], kv_end, swap_wide, [grad_down]
    )

    kv_climb = Climb(sum_last(kv_blocks, kv_end).astype(BF))
    moving = advance([kv_climb, out_climb, query_climb])
    mixed_mid = sum_first(mixed_blocks)
    wide_done = [[c.value, s] for c, s in zip(climbs, swap_wide)]
    grad_gate_w, grad_up_w = place_wide(wide_done)
    take([kv_climb, out_climb, query_climb], moving)
    mixed_mid, (grad_gate_w, grad_up_w) = sync_climbs(
        [kv_climb, out_climb, query_climb], mixed_mid, [grad_gate_w, grad_up_w]
    )

    moving = advance([query_climb, kv_climb])
    mixed_end = sum_second(mixed_blocks, mixed_mid)
    out_done = [complete(out_climb).value, swap_run(out_climb.value, 1)]
    (grad_out_w,) = put(both_rows(out_done, 0, model_width, 0), [(shard, model_width)])
    take([query_climb, kv_climb], moving)
    mixed_end, (grad_out_w,) = sync_climbs([query_climb, kv_climb], mixed_end, [grad_out_w])
    mixed_sum = sum_last(mixed_blocks, mixed_end)
    output = (residual + mixed_sum).astype(BF).reshape(seq_count, tok_count, model_width)
    query_done, kv_done = [
        [c.value, swap_run(c.value, 1)] for c in [complete(c) for c in (query_climb, kv_climb)]
    ]
    grad_query_w, grad_key_w, grad_value_w, gain_out = put(
        both_rows(query_done, 0, model_width, 0)
        + both_rows(kv_done, 0, KW, 1)
        + both_rows(kv_done, KW, KW, 2)
        + both_rows(kv_done, 2 * KW, 128, 3),
        [(shard, model_width), (shard, KW), (shard, KW), (shard, 128)],
    )
    return (
        output,
        grad_in,
        gain_out[:, 0],
        grad_query_w,
        grad_key_w,
        grad_value_w,
        grad_out_w,
        gain_out[:, 1],
        grad_gate_w,
        grad_up_w,
        grad_down,
    )


def solution(mesh):
    placed = (
        P("fsdp", "ctx", None),
        P("fsdp", "ctx"),
        P("fsdp", "ctx", None),
        P("fsdp"),
        P("fsdp", None),
        P("fsdp", None),
        P("fsdp", None),
        P("fsdp", None),
        P("fsdp"),
        P("fsdp", None),
        P("fsdp", None),
        P("fsdp", None),
    )
    return jax.shard_map(
        on_device,
        mesh=mesh,
        in_specs=placed,
        out_specs=(
            P("fsdp", "ctx", None),
            P("fsdp", "ctx", None),
            P("fsdp"),
            P("fsdp", None),
            P("fsdp", None),
            P("fsdp", None),
            P("fsdp", None),
            P("fsdp"),
            P("fsdp", None),
            P("fsdp", None),
            P("fsdp", None),
        ),
        check_vma=False,
    )
```

```python
import functools

import jax
import jax.numpy as jnp
from jax import lax
from jax.experimental import pallas as pl
from jax.experimental.pallas import tpu as pltpu
from jax.sharding import PartitionSpec as P

H = 32
KVH = 4
HD = 64
GROUP = H // KVH
KW = KVH * HD


NORM_EPS = 1e-05
MASKED = -1e30
BF = jnp.bfloat16
F32 = jnp.float32
ROOM = 60 * 1024 * 1024
EXTRA = 16


def rms_scale(inputs):
    return lax.rsqrt(jnp.mean(inputs * inputs, -1, keepdims=True) + NORM_EPS)


def norm_back(grad_normed, inputs, row_scale, gain_row):
    scaled_grad = grad_normed * gain_row
    grad_gain = jnp.sum(grad_normed * inputs * row_scale, 0)
    grad_inputs = row_scale * scaled_grad - inputs * row_scale**3 * jnp.mean(
        scaled_grad * inputs, -1, keepdims=True
    )
    return (grad_inputs, grad_gain)


def at(array, start, size, axis=0):
    return lax.dynamic_slice_in_dim(array, start, size, axis)


def dot(a, b):
    return jnp.dot(a, b, preferred_element_type=F32)


def dot_cols(a, b):
    return lax.dot_general(a, b, (((1,), (1,)), ((), ())), preferred_element_type=F32)


def dot_rows(a, b):
    return lax.dot_general(a, b, (((0,), (0,)), ((), ())), preferred_element_type=F32)


def swap_halves(value):
    lane = lax.broadcasted_iota(jnp.int32, value.shape, 1)
    size = value.shape[1]
    ahead = pltpu.roll(value, size - HD // 2, 1)
    behind = pltpu.roll(value, HD // 2, 1)
    return jnp.where(lane % HD < HD // 2, ahead, behind)


def spin(value, cosine, sine):
    return value * cosine + swap_halves(value) * sine


def call(
    body, outs, args, scratch=(), flops=0, nbytes=0, grid=None, in_specs=None, out_specs=None,
    after=(), prefetch=False,
):
    whole = pl.BlockSpec(memory_space=pltpu.VMEM)
    many = isinstance(outs, (list, tuple))
    in_specs = list(in_specs or [whole] * len(args))
    count = len(args)
    args = [*args, *after]
    in_specs += [pl.BlockSpec(memory_space=pl.ANY)] * len(after)

    def run(*refs):
        return body(*refs[:count], *refs[count + len(after) :])

    options = pltpu.CompilerParams(vmem_limit_bytes=ROOM)
    cost = pl.CostEstimate(flops=flops, bytes_accessed=nbytes, transcendentals=0)
    if prefetch:
        return pl.pallas_call(
            run,
            out_shape=outs,
            grid_spec=pltpu.PrefetchScalarGridSpec(
                num_scalar_prefetch=1, grid=grid, in_specs=in_specs, out_specs=out_specs
            ),
            compiler_params=options,
            cost_estimate=cost,
        )(*args)
    return pl.pallas_call(
        run,
        out_shape=outs,
        in_specs=in_specs,
        out_specs=out_specs or ([whole] * len(outs) if many else whole),
        scratch_shapes=list(scratch),
        grid=grid or (),
        compiler_params=options,
        cost_estimate=cost,
    )(*args)


def shape(dims, kind):
    return jax.ShapeDtypeStruct(tuple(dims), kind)


class Pieces:
    def __init__(self, own, sources, blocks, cell, width, levels=0):
        self.levels = levels
        self.own, self.sources, self.blocks = list(own), list(sources), tuple(blocks)
        self.cell, self.width = cell, width
        self.part_rows = own[0].shape[0]
        self.count = len(self.own) + len(self.sources)
        self.copies = len(self.own) + len(self.blocks)

    def args(self):
        return self.own + self.sources

    def spot(self, where, step, flip):
        side = where[2] ^ flip
        if self.levels:
            side = lax.rem(where[3] + self.levels - step, self.levels) * 2 + side
        return pl.multiple_of(side * self.cell, self.cell)

    def row(self, where, row, bit):
        return row if row is not None else pl.multiple_of((where[0] ^ bit) * self.cell, self.cell)

    def moves(self, where, refs, bit, first, size):
        own, sources = refs[: len(self.own)], refs[len(self.own) :]
        step = self.width // len(self.own)
        moves = []
        if bit == 0:
            for number, source in enumerate(own):
                column = first
                if len(own) > 1:
                    column = pl.multiple_of(where[0] * step + first, 128)
                moves.append((source.at[:, pl.ds(column, size)], 0, self.part_rows, number))
        for source, row, step_, flip, flag in self.blocks:
            if flag != bit:
                continue
            spot = self.spot(where, step_, flip)
            for number in range(len(own)):
                row_ = self.row(where, row, bit)
                place = sources[source].at[
                    pl.ds(row_, self.cell), pl.ds(number * step + first, size)
                ]
                moves.append((place, spot, self.cell, number))
        return moves

    def whole_moves(self, where, refs, bit):
        own, sources = refs[: len(self.own)], refs[len(self.own) :]
        step = self.width // len(self.own)
        moves = []
        if bit == 0:
            for number, source in enumerate(own):
                column = pl.multiple_of(where[0] * step, 128) if len(own) > 1 else 0
                moves.append(
                    (source.at[:, pl.ds(column, step)], 0, self.part_rows, number * step, step)
                )
        for source, row, step_, flip, flag in self.blocks:
            if flag == bit:
                spot = self.spot(where, step_, flip)
                moves.append(
                    (
                        sources[source].at[pl.ds(self.row(where, row, bit), self.cell), :],
                        spot,
                        self.cell,
                        0,
                        self.width,
                    )
                )
        return moves


def fetch_parts(pieces, where, refs, held, sems, parts):
    groups, number = [], 0
    for bit in range(parts):
        group = []
        for source, row, rows, column, cols in pieces.whole_moves(where, refs, bit):
            target = held.at[bit, pl.ds(row, rows), pl.ds(column, cols)]
            copy = pltpu.make_async_copy(source, target, sems.at[number])
            copy.start()
            group.append(copy)
            number += 1
        groups.append(group)
    return groups


SMEM = pl.BlockSpec(memory_space=pltpu.SMEM)
VMEM = pl.BlockSpec(memory_space=pltpu.VMEM)
HBM = pl.BlockSpec(memory_space=pl.ANY)


def forward_body(pieces, parts, where, left_ref, *refs):
    (out_ref, held, sems), refs = refs[-3:], refs[:-3]
    groups = fetch_parts(pieces, where, refs, held, sems, parts)
    rows = pieces.part_rows
    chunk = min(512, pieces.width)
    for bit in range(parts):
        for copy in groups[bit]:
            copy.wait()
        first = pl.multiple_of((where[0] ^ bit) * rows, 128)
        left = left_ref[:, pl.ds(first, rows)]

        def step(number, carry, bit=bit, left=left):
            cols = pl.ds(pl.multiple_of(number * chunk, chunk), chunk)
            part = dot(left, held[bit, :, cols])
            out_ref[:, cols] = part if bit == 0 else out_ref[:, cols] + part
            return carry

        lax.fori_loop(0, pieces.width // chunk, step, 0)


def forward_mm(where, left, pieces, parts, after=()):
    rows, depth = left.shape
    return call(
        functools.partial(forward_body, pieces, parts),
        shape((rows, pieces.width), F32),
        [where, left, *pieces.args()],
        [
            pltpu.VMEM((parts, pieces.part_rows, pieces.width), BF),
            pltpu.SemaphoreType.DMA((pieces.copies,)),
        ],
        flops=2 * rows * depth * pieces.width,
        nbytes=2 * (rows * depth + depth * pieces.width + 2 * rows * pieces.width),
        in_specs=[SMEM, VMEM] + [HBM] * pieces.count,
        after=after,
    )


def back_body(pieces, parts, blocks, where, left_ref, *refs):
    outs, (held, sems), refs = refs[-2 - blocks : -2], refs[-2:], refs[: -2 - blocks]
    groups = fetch_parts(pieces, where, refs, held, sems, parts)
    rows = pieces.part_rows
    chunk = min(256, rows)
    tall = outs[0].shape[0]
    for bit in range(parts):
        for copy in groups[bit]:
            copy.wait()

        def step(number, carry, bit=bit):
            spot = pl.ds(pl.multiple_of(number * chunk, chunk), chunk)
            weight = held[bit, spot, :]
            first = pl.multiple_of((where[0] ^ bit) * rows + number * chunk, 128)
            for block, out_ref in enumerate(outs):
                left = left_ref[block * tall : (block + 1) * tall, :]
                out_ref[:, pl.ds(first, chunk)] = dot_cols(left, weight).astype(out_ref.dtype)
            return carry

        lax.fori_loop(0, rows // chunk, step, 0)


def back_mm(where, left, pieces, parts, kind, blocks=1, after=()):
    rows, depth = left.shape
    width = parts * pieces.part_rows
    return call(
        functools.partial(back_body, pieces, parts, blocks),
        [shape((rows // blocks, width), kind)] * blocks,
        [where, left, *pieces.args()],
        [
            pltpu.VMEM((parts, pieces.part_rows, pieces.width), BF),
            pltpu.SemaphoreType.DMA((pieces.copies,)),
        ],
        flops=2 * rows * depth * width,
        nbytes=2 * (rows * depth + depth * width + rows * width),
        in_specs=[SMEM, VMEM] + [HBM] * pieces.count,
        after=after,
    )


def spans_of(width):
    groups = [(first, min(512, width - first)) for first in range(0, width, 512)]
    return [
        (first, size, [(at_, min(256, size - at_)) for at_ in range(0, size, 256)])
        for first, size in groups
    ]


def feed_body(pieces, parts, counts, where, *refs):
    tokens, refs = refs[: counts[0]], refs[counts[0] :]
    grads, refs = refs[: counts[1]], refs[counts[1] :]
    down_ref, refs = refs[0], refs[1:]
    weights, refs = refs[: pieces.count], refs[pieces.count :]
    hid_ref, wide_ref, normed, grad, wide_w, down_w, sems = refs
    cols = pieces.width // 2
    number = 0

    def go(source, target):
        nonlocal number
        copy = pltpu.make_async_copy(source, target, sems.at[number])
        copy.start()
        number += 1
        return copy

    def stack(sources, target):
        row, copies = 0, []
        for source in sources:
            rows = source.shape[0]
            copies.append(go(source, target.at[pl.ds(row, rows), :]))
            row += rows
        return copies

    first_copies = stack(tokens, normed)
    groups = []
    for first, size, _ in spans_of(cols):
        group = []
        for bit in range(parts):
            base = pl.multiple_of((where[0] ^ bit) * pieces.part_rows, pieces.cell)
            for source, row, rows, side in pieces.moves(where, weights, bit, first, size):
                spot = pl.multiple_of(base + row, pieces.cell)
                target = wide_w.at[pl.ds(spot, rows), pl.ds(side * cols + first, size)]
                group.append(go(source, target))
        group.append(go(down_ref.at[pl.ds(first, size), :], down_w.at[pl.ds(first, size), :]))
        groups.append(group)
        if first == 0:
            first_copies += stack(grads, grad)
    for copy in first_copies:
        copy.wait()
    total = normed.shape[0]
    tall = min(512, total)
    for (first, size, pieces_), group in zip(spans_of(cols), groups):
        for copy in group:
            copy.wait()
        for offset, width in pieces_:
            left = first + offset
            gate_cols = slice(left, left + width)
            up_cols = slice(cols + left, cols + left + width)

            def step(block, carry, gate_cols=gate_cols, up_cols=up_cols):
                rows = pl.ds(pl.multiple_of(block * tall, tall), tall)
                gate = dot(normed[rows, :], wide_w[:, gate_cols])
                up = dot(normed[rows, :], wide_w[:, up_cols])
                back = dot_cols(grad[rows, :], down_w[gate_cols, :])
                sig = 1.0 / (1.0 + jnp.exp(-gate))
                silu = gate * sig
                hid_ref[rows, gate_cols] = (silu * up).astype(BF)
                wide_ref[rows, up_cols] = (back * silu).astype(BF)
                slope = sig * (1.0 + gate * (1.0 - sig))
                wide_ref[rows, gate_cols] = (back * up * slope).astype(BF)
                return carry

            lax.fori_loop(0, total // tall, step, 0)


def feed(where, tokens, grads, down, pieces, parts):
    rows = sum(a.shape[0] for a in tokens)
    depth = tokens[0].shape[1]
    cols = pieces.width // 2
    copies = len(tokens) + len(grads)
    copies += len(spans_of(cols)) * (2 * pieces.copies + 1)
    return call(
        functools.partial(feed_body, pieces, parts, (len(tokens), len(grads))),
        [
            shape((rows, cols), BF),
            shape((rows, 2 * cols), BF),
            shape((rows, depth), BF),
            shape((rows, depth), BF),
        ],
        [where, *tokens, *grads, down, *pieces.args()],
        [
            pltpu.VMEM((depth, 2 * cols), BF),
            pltpu.VMEM((cols, depth), BF),
            pltpu.SemaphoreType.DMA((copies,)),
        ],
        flops=6 * rows * depth * cols,
        nbytes=6 * depth * cols + 4 * rows * depth + 6 * rows * cols,
        in_specs=[SMEM] + [HBM] * (len(tokens) + len(grads) + 1 + pieces.count),
    )


def grad_body(parts, gots, outs, where, left_ref, right_ref, *refs):
    total = dot_rows(left_ref[...], right_ref[...])
    half = left_ref.shape[1]
    for number in range(parts):

        @pl.when(pl.program_id(0) == number)
        def _(number=number):
            value = total
            if gots:
                value = value.astype(BF).astype(F32)
                value = value + refs[number * gots // parts][...].astype(F32)
            per = parts // outs
            out_ref = refs[gots + number // per]
            row = number % per * half
            out_ref[row : row + half, :] = value.astype(BF)


def grad_mm(where, left, right, side, parts, got=(), after=(), outs=1):
    rows, depth = left.shape
    width = right.shape[1]
    half = depth // parts // 2
    gots = len(got)
    column = lambda b, w: (0, (w[0] ^ b) * 2 + (w[2] ^ side))

    def piece(number):
        per = parts // gots
        return pl.BlockSpec(
            (half, width), lambda b, w: (jnp.clip(b - number * per, 0, per - 1), 0)
        )

    tall = parts // outs * half
    made = call(
        functools.partial(grad_body, parts, gots, outs),
        [shape((tall, width), BF)] * outs,
        [where, left, right, *got],
        flops=2 * rows * parts * half * width,
        nbytes=2 * (rows * parts * half + rows * width + parts * half * width),
        grid=(parts,),
        in_specs=[
            pl.BlockSpec((rows, half), column),
            pl.BlockSpec((rows, width), lambda b, w: (0, 0)),
        ]
        + [piece(number) for number in range(gots)],
        out_specs=[pl.BlockSpec((tall, width), lambda b, w: (0, 0))] * outs,
        after=after,
        prefetch=True,
    )
    return made


def mix_body(apart, left_ref, right_ref, *outs):
    total = dot(left_ref[...], right_ref[...]).astype(BF)
    for number in range(apart):

        @pl.when(pl.program_id(0) == number)
        def _(number=number):
            outs[number][...] = total


def mix(left, right, blocks, after=()):
    rows, depth = left.shape
    width = right.shape[1]
    tall = rows // blocks
    return call(
        functools.partial(mix_body, blocks),
        [shape((tall, width), BF)] * blocks,
        [left, right],
        flops=2 * rows * depth * width,
        nbytes=2 * (rows * depth + depth * width + rows * width),
        grid=(blocks,),
        in_specs=[
            pl.BlockSpec((tall, depth), lambda n: (n, 0)),
            pl.BlockSpec((depth, width), lambda n: (0, 0)),
        ],
        out_specs=[pl.BlockSpec((tall, width), lambda n: (0, 0))] * blocks,
        after=after,
    )


def key_value_body(pieces, parts, where, x_ref, gain_ref, cos_ref, sin_ref, tag_ref, *refs):
    (normed_ref, out_ref, held, sems), refs = refs[-4:], refs[:-4]
    groups = fetch_parts(pieces, where, refs, held, sems, parts)
    x = x_ref[...].astype(F32)
    normed_ref[...] = (x * rms_scale(x) * gain_ref[0:1, :]).astype(BF)
    rows = x.shape[0]
    both = 0.0
    for bit in range(parts):
        for copy in groups[bit]:
            copy.wait()
        first = pl.multiple_of((where[0] ^ bit) * pieces.part_rows, 128)
        both = both + dot(normed_ref[:, pl.ds(first, pieces.part_rows)], held[bit])
    cosine = jnp.concatenate([cos_ref[...]] * (KW // 128), 1)
    sine = jnp.concatenate([sin_ref[...]] * (KW // 128), 1)
    keys = spin(both[:, :KW], cosine, sine)
    out_ref[:rows, :KW] = keys.astype(BF)
    out_ref[:rows, KW:] = both[:, KW:].astype(BF)
    out_ref[rows:, :] = tag_ref[...]


def seq_keys(kv_refs, seq, head, tok):
    rows = pl.ds(seq * tok, tok)
    found = []
    for first in (head * HD, KW + head * HD):
        sides = [ref[:, rows, first : first + HD].reshape(-1, HD) for ref in kv_refs]
        found.append(jnp.concatenate(sides, 0))
    return found


def fill_bias(kv_refs, tag_ref, bias_ref, seq, tok, rows):
    levels = kv_refs[0].shape[0]
    row = lax.broadcasted_iota(jnp.int32, (EXTRA, 128), 0)

    def start_of(block):
        return jnp.sum(jnp.where(row == seq, block.astype(F32), 0.0), 0, keepdims=True)

    own = start_of(tag_ref[:, 0:128])
    ahead = (
        lax.broadcasted_iota(jnp.int32, (tok, 128), 0)
        - lax.broadcasted_iota(jnp.int32, (tok, 128), 1)
    ).astype(F32)
    for run in range(2 * levels):
        tags = kv_refs[run // levels][run % levels, rows : rows + EXTRA, 0:128]
        lead = (start_of(tags) - own) * float(tok)
        block = jnp.where(ahead + lead <= 0.0, 0.0, MASKED)
        bias_ref[run * tok : (run + 1) * tok, :] = jnp.concatenate([block, block], 1)


def stack_heads(two):
    return jnp.concatenate([two[:, :HD], two[:, HD:]], 0)


def lay_heads(stacked):
    tok = stacked.shape[0] // 2
    return jnp.concatenate([stacked[:tok], stacked[tok:]], 1)


def attend_body(seq, q_ref, kept_ref, other_ref, tag_ref, cos_ref, sin_ref, rot_ref, out_ref, log_ref, bias_ref):
    tok = q_ref.shape[0]
    kv_refs = (kept_ref, other_ref)
    rows = kept_ref.shape[1] - EXTRA
    fill_bias(kv_refs, tag_ref, bias_ref, seq, tok, rows)
    for head in range(KVH):
        keys, values = seq_keys(kv_refs, seq, head, tok)
        values_t = values.astype(F32).T.astype(BF)

        def pair(number, carry, head=head, keys=keys, values_t=values_t):
            first = head * GROUP + 2 * number
            lanes = pl.ds(pl.multiple_of(first * HD, 128), 128)
            turned = spin(q_ref[:, lanes], cos_ref[...], sin_ref[...]).astype(BF)
            turned = turned * jnp.asarray(HD**-0.5, BF)
            rot_ref[:, lanes] = turned
            scores = dot_cols(keys, stack_heads(turned)) + bias_ref[...]
            top = jnp.max(scores, 0, keepdims=True)
            weights = jnp.exp(scores - top)
            total = jnp.sum(weights, 0, keepdims=True)
            shares = (weights * (1.0 / total)).astype(BF)
            mixed = dot(values_t, shares).T
            out_ref[:, lanes] = lay_heads(mixed).astype(BF)
            logs = top + jnp.log(total)
            log_ref[0, pl.ds(first, 1), :] = logs[:, :tok]
            log_ref[0, pl.ds(first + 1, 1), :] = logs[:, tok:]
            return carry

        lax.fori_loop(0, GROUP // 2, pair, 0)


def attend(seq, query_raw, kv, tag, cosine, sine, tok, after=()):
    width = query_raw.shape[1]
    runs = 2 * kv[0].shape[0]
    block = pl.BlockSpec((tok, width), lambda s: (seq, 0))
    table = pl.BlockSpec((tok, 128), lambda s: (seq, 0))
    fixed = lambda dims: pl.BlockSpec(dims, lambda s: (0,) * len(dims))
    return call(
        functools.partial(attend_body, seq),
        [shape((tok, width), BF), shape((tok, width), BF), shape((1, H, tok), F32)],
        [query_raw, *kv, tag, cosine, sine],
        [pltpu.VMEM((runs * tok, 2 * tok), F32)],
        flops=16 * H * tok * runs * tok * HD,
        nbytes=tok * width * 8,
        grid=(1,),
        in_specs=[block, fixed(kv[0].shape), fixed(kv[0].shape), fixed(tag.shape), table, table],
        out_specs=[fixed((tok, width)), fixed((tok, width)), fixed((1, H, tok))],
        after=after,
    )


def attend_back_body(
    seq, heads, rot_ref, kept_ref, other_ref, tag_ref, log_ref, grad_ref, cos_ref, sin_ref, dq_ref,
    dkept_ref, dother_ref, bias_ref, dk_ref, dv_ref,
):
    tok = rot_ref.shape[0]
    kv_refs = (kept_ref, other_ref)
    rows = kept_ref.shape[1] - EXTRA
    levels = kept_ref.shape[0]
    fill_bias(kv_refs, tag_ref, bias_ref, seq, tok, rows)
    for head in heads:
        keys, values = seq_keys(kv_refs, seq, head, tok)
        keys_t = keys.astype(F32).T.astype(BF)
        dk_ref[...] = jnp.zeros_like(dk_ref)
        dv_ref[...] = jnp.zeros_like(dv_ref)

        def pair(number, carry, head=head, keys=keys, values=values, keys_t=keys_t):
            first = head * GROUP + 2 * number
            lanes = pl.ds(pl.multiple_of((first - heads[0] * GROUP) * HD, 128), 128)
            queries = stack_heads(rot_ref[:, lanes])
            grads = stack_heads(grad_ref[:, lanes])
            logs = jnp.concatenate(
                [log_ref[0, pl.ds(first, 1), :], log_ref[0, pl.ds(first + 1, 1), :]], 1
            )
            shares = jnp.exp(dot_cols(keys, queries) + bias_ref[...] - logs)
            grad_shares = dot_cols(values, grads)
            inner = jnp.sum(shares * grad_shares, 0, keepdims=True)
            grad_scores = (shares * (grad_shares - inner)).astype(BF)
            dk_ref[...] += dot(grad_scores, queries)
            dv_ref[...] += dot(shares.astype(BF), grads)
            grad_q = (dot(keys_t, grad_scores) * HD**-0.5).T
            grad_q = spin(lay_heads(grad_q), cos_ref[...], -sin_ref[...])
            dq_ref[:, lanes] = grad_q.astype(BF)
            return carry

        lax.fori_loop(0, GROUP // 2, pair, 0)
        low, high = (head - heads[0]) * HD, (head - heads[0] + 1) * HD
        step = len(heads) * HD
        for side, out_ref in enumerate((dkept_ref, dother_ref)):
            span = slice(side * levels * tok, (side + 1) * levels * tok)
            out_ref[:, :, low:high] = dk_ref[span, :].astype(BF).reshape(levels, tok, HD)
            out_ref[:, :, step + low : step + high] = (
                dv_ref[span, :].astype(BF).reshape(levels, tok, HD)
            )


def attend_back(seq, heads, rot, kv, tag, logs, grad, cosine, sine, tok, after=()):
    width = len(heads) * GROUP * HD
    lane = heads[0] // len(heads)
    runs = 2 * kv[0].shape[0]
    table = pl.BlockSpec((tok, 128), lambda s: (seq, 0))
    fixed = lambda dims: pl.BlockSpec(dims, lambda s: (0,) * len(dims))
    moved = (runs // 2, tok, 2 * len(heads) * HD)
    return call(
        functools.partial(attend_back_body, seq, heads),
        [shape((tok, width), BF)] + [shape(moved, BF)] * 2,
        [rot, *kv, tag, logs, grad, cosine, sine],
        [
            pltpu.VMEM((runs * tok, 2 * tok), F32),
            pltpu.VMEM((runs * tok, HD), F32),
            pltpu.VMEM((runs * tok, HD), F32),
        ],
        flops=10 * len(heads) * GROUP * tok * runs * tok * HD,
        nbytes=tok * width * 8,
        grid=(1,),
        in_specs=[
            pl.BlockSpec((tok, width), lambda s: (0, lane)),
            fixed(kv[0].shape),
            fixed(kv[0].shape),
            fixed(tag.shape),
            fixed((1, H, tok)),
            pl.BlockSpec((tok, width), lambda s: (seq, lane)),
            table,
            table,
        ],
        out_specs=[fixed((tok, width))] + [fixed(moved)] * 2,
        after=after,
    )


def kv_back_body(*refs):
    parts, (cos_ref, sin_ref, out_ref) = refs[:-3], refs[-3:]
    total = parts[0][...].astype(F32)
    for part in parts[1:]:
        total = total + part[...].astype(F32)
    cosine = jnp.concatenate([cos_ref[...]] * (KW // 128), 1)
    sine = jnp.concatenate([sin_ref[...]] * (KW // 128), 1)
    out_ref[:, :KW] = spin(total[:, :KW], cosine, -sine).astype(BF)
    out_ref[:, KW:] = total[:, KW:].astype(BF)


def place_body(plan, count, outs, where, *refs):
    pieces, targets = refs[:count], refs[count : count + outs]
    held, wide, in_sems, out_sems = refs[count + outs :]
    mine, core = where[0], where[2]
    reads, writes = [], []
    for number, (piece, first, column, rows, cols, target, place) in enumerate(plan):
        slot = number % 2
        top, left = place(mine, core)
        reads.append(
            pltpu.make_async_copy(
                pieces[piece].at[pl.ds(first, rows), pl.ds(column, cols)],
                held.at[slot, pl.ds(0, rows), pl.ds(0, cols)],
                in_sems.at[slot],
            )
        )
        writes.append(
            pltpu.make_async_copy(
                wide.at[slot, pl.ds(0, rows), pl.ds(0, cols)],
                targets[target].at[pl.ds(top, rows), pl.ds(left, cols)],
                out_sems.at[slot],
            )
        )
    reads[0].start()
    for number, (_, _, _, rows, cols, _, _) in enumerate(plan):
        slot = number % 2
        if number + 1 < len(plan):
            reads[number + 1].start()
        reads[number].wait()
        if number >= 2:
            writes[number - 2].wait()
        wide[slot, :rows, :cols] = held[slot, :rows, :cols].astype(F32)
        writes[number].start()
    for copy in writes[-2:]:
        copy.wait()


def place(where, pieces, plan, outs):
    hbm = pl.BlockSpec(memory_space=pl.ANY)
    rows = max(step[3] for step in plan)
    cols = max(step[4] for step in plan)
    moved = sum(step[3] * step[4] for step in plan)
    return call(
        functools.partial(place_body, plan, len(pieces), len(outs)),
        [shape(dims, F32) for dims in outs],
        [where, *pieces],
        [
            pltpu.VMEM((2, rows, cols), BF),
            pltpu.VMEM((2, rows, cols), F32),
            pltpu.SemaphoreType.DMA((2,)),
            pltpu.SemaphoreType.DMA((2,)),
        ],
        nbytes=6 * moved,
        in_specs=[pl.BlockSpec(memory_space=pltpu.SMEM)] + [hbm] * len(pieces),
        out_specs=[hbm] * len(outs),
    )


def on_device(
    hidden_in,
    positions,
    cotangent,
    norm_gain,
    w_query,
    w_key,
    w_value,
    w_out,
    ffn_gain,
    w_gate,
    w_up,
    w_down,
):
    seq_count, tok_count, model_width = hidden_in.shape
    row_count = seq_count * tok_count
    parts = lax.axis_size("fsdp")
    runs = lax.axis_size("ctx")
    levels = runs // 2
    mine = lax.axis_index("fsdp").astype(jnp.int32)
    run = lax.axis_index("ctx").astype(jnp.int32)
    core = lax.rem(run, 2)
    level = run // 2
    quarter = lax.rem(run, 4)
    where = jnp.stack([mine, quarter, core, level])
    shard = model_width // parts
    half = shard // 2
    ff_part = w_down.shape[0]
    aligned = ff_part % 128 == 0

    def hop(array, bit):
        return lax.ppermute(array, "fsdp", [(i, i ^ bit) for i in range(parts)])

    def swap_run(array, bit):
        return lax.ppermute(array, "ctx", [(i, i ^ bit) for i in range(runs)])

    def level_send(array, pairs):
        return lax.ppermute(
            array, "ctx", [(2 * a + k, 2 * b + k) for a, b in pairs for k in range(2)]
        )

    def tie(values, *after):
        many = isinstance(values, (list, tuple))
        flat = list(values) if many else [values]
        tied = lax.optimization_barrier((*flat, *after))[: len(flat)]
        return list(tied) if many else tied[0]

    def add(a, b):
        return (a.astype(F32) + b.astype(F32)).astype(BF)

    def spread(local):
        if parts != 4:
            return [hop(local, bit) for bit in range(1, parts)]
        middle = local.shape[0] // 2
        from_x, from_y = hop(local, 1), hop(local, 2)
        return [from_x, from_y, hop(from_x[:middle], 2), hop(from_y[middle:], 1)]

    def halves(own, pieces, others, width):
        cell = own[0].shape[0] // 2
        blocks = [(bit - 1, 0, 0, 0, bit) for bit in range(1, parts)]
        bit = 1
        for number, other in enumerate(others):
            for row in range(0, other.shape[0], cell):
                blocks.append((parts - 1 + number, row, 0, 1, bit))
                bit += 1
        return Pieces(own, pieces + list(others), blocks, cell, width)

    def swap_all(arrays):
        return [swap_run(a, 1) for a in arrays]

    def hops(local):
        return [hop(local, bit) for bit in range(1, parts)]

    def turn(array):
        return level_send(array, [(i, (i + 1) % levels) for i in range(levels)])

    def columns_of(sources, index, cols):
        cell = sources[0].shape[0] // runs
        return jnp.concatenate(
            [lax.dynamic_slice(a, (run * cell, index * cols), (cell, cols)) for a in sources],
            1,
        )

    def lay_rows(pieces):
        rows, cell, width = pieces.part_rows, pieces.cell, pieces.width
        step = width // len(pieces.own)
        local = jnp.concatenate([at(a, mine * step, step, 1) for a in pieces.own], 1)
        whole = jnp.zeros((parts * rows, width), BF)
        whole = lax.dynamic_update_slice(whole, local, (mine * rows, 0))
        for source, first, back, flip, bit in pieces.blocks:
            side = lax.rem(level + levels - back, levels) * 2 + (core ^ flip)
            spot = (mine ^ bit) * rows + side * cell
            piece = pieces.sources[source][first : first + cell]
            whole = lax.dynamic_update_slice(whole, piece, (spot, 0))
        return whole

    def sum_first(blocks):
        if parts != 4:
            return [hop(blocks[bit], bit) for bit in range(1, parts)]
        middle = blocks[0].shape[0] // 2
        return [hop(blocks[3][middle:], 1), hop(blocks[3][:middle], 2)]

    def sum_second(blocks, got):
        if parts != 4:
            return got
        middle = blocks[0].shape[0] // 2
        to_x = jnp.concatenate([add(blocks[1][:middle], got[1]), blocks[1][middle:]], 0)
        to_y = jnp.concatenate([blocks[2][:middle], add(blocks[2][middle:], got[0])], 0)
        return [hop(to_x, 1), hop(to_y, 2)]

    def sum_last(blocks, got):
        return sum([a.astype(F32) for a in got], blocks[0].astype(F32))

    def far_of(pieces):
        if parts != 4:
            return []
        half_ = pieces[0].shape[0] // 2
        return [hop(pieces[0][:half_], 2), hop(pieces[1][half_:], 1)]

    def near_of(local):
        return [hop(local, bit) for bit in ((1, 2) if parts == 4 else range(1, parts))]

    middle_level = levels // 2
    last_level = levels - 1
    ups = [[(s, s + 1), (last_level - s, last_level - s - 1)] for s in range(middle_level - 1)]
    over = [(middle_level - 1, middle_level), (middle_level, middle_level - 1)]
    downs = [[(b, a) for a, b in pairs] for pairs in reversed(ups)]

    class Climb:
        def __init__(self, value):
            self.value, self.stage = value, 0

        def start(self):
            self.moving = level_send(self.value, (ups + [over] + downs)[self.stage])
            return self.moving

        def take(self, got):
            if self.stage < middle_level:
                self.value = add(self.value, got)
            else:
                s = 2 * middle_level - 2 - self.stage
                ends = (level == s) | (level == last_level - s)
                self.value = jnp.where(ends, got, self.value)
            self.stage += 1

        @property
        def done(self):
            return self.stage == 2 * middle_level - 1

    def complete(climb):
        while not climb.done:
            climb.take(climb.start())
        return climb

    def both_ways(new, old):
        if levels != 4 or new.value.shape != old.value.shape:
            return [new.start(), old.start()]
        inner = (level == 1) | (level == 2)
        sent = jnp.where(inner, old.value, new.value)
        return [level_send(sent, [(0, 1), (1, 0), (2, 3), (3, 2)])]

    def take_both(new, old, got):
        if len(got) == 2:
            new.take(got[0])
            old.take(got[1])
            return
        inner = (level == 1) | (level == 2)
        new.value = jnp.where(inner, add(new.value, got[0]), new.value)
        old.value = jnp.where(inner, old.value, got[0])
        new.stage += 1
        old.stage += 1

    def advance(climbs):
        return [c.start() for c in climbs]

    def take(climbs, results):
        for climb, got in zip(climbs, results):
            climb.take(got)

    def values(climbs):
        return [c.value for c in climbs]

    def sync(*groups):
        flat = [a for group in groups for a in group]
        flat = list(lax.optimization_barrier(tuple(flat)))
        out = []
        for group in groups:
            out.append(flat[: len(group)])
            flat = flat[len(group) :]
        return out

    def sync_climbs(climbs, *groups):
        held, *rest = sync(values(climbs), *groups)
        for climb, value in zip(climbs, held):
            climb.value = value
        return rest

    gains = jnp.stack([norm_gain, ffn_gain] + [jnp.zeros_like(norm_gain)] * (EXTRA - 2), 0)
    own_kv = jnp.concatenate([w_key, w_value], 1)
    wide = own_kv.shape[1] // shard
    tag_rows = jnp.concatenate([gains] * wide, 1)
    sent_kv = jnp.concatenate([at(own_kv, core * half, half), tag_rows], 0)
    got_kv = [hop(sent_kv, bit) for bit in range(1, parts)]
    own_query = at(w_query, core * half, half)
    got_kv[:1], (own_query,) = sync(got_kv[:1], [own_query])
    near_query = [hop(own_query, bit) for bit in range(1, min(3, parts))]
    got_kv = tie(got_kv)
    kv_pieces = [a[:half] for a in got_kv]
    other_kv = swap_run(jnp.concatenate(kv_pieces, 0), 1)
    rest_query = [hop(tie(own_query, *got_kv), bit) for bit in range(3, parts)]
    key_value_w = halves([own_kv], kv_pieces, [other_kv], own_kv.shape[1])
    gain_cells = [gains] + [a[half:, :shard] for a in got_kv]
    all_gains = jnp.zeros((EXTRA, model_width), BF)
    for bit in range(parts):
        all_gains = lax.dynamic_update_slice(
            all_gains, gain_cells[bit], (0, (mine ^ bit) * shard)
        )
    all_gains = all_gains.astype(F32)
    gain_one, gain_two = all_gains[0], all_gains[1]

    spread_of = 10000.0 ** (-jnp.arange(HD // 2, dtype=F32) / (HD // 2))
    turned = positions.astype(F32).reshape(row_count, 1) * spread_of
    cosine = jnp.concatenate([jnp.cos(turned)] * 4, 1)
    sine = jnp.concatenate([-jnp.sin(turned), jnp.sin(turned)] * 2, 1)
    starts = (positions[:, :1] // tok_count).astype(BF)
    tag = jnp.concatenate(
        [
            jnp.broadcast_to(starts, (seq_count, 2 * KW)),
            jnp.zeros((EXTRA - seq_count, 2 * KW), BF),
        ],
        0,
    )

    x_low = hidden_in.reshape(row_count, model_width)
    normed_one, packed = call(
        functools.partial(key_value_body, key_value_w, parts),
        [shape((row_count, model_width), BF), shape((row_count + EXTRA, 2 * KW), BF)],
        [where, x_low, all_gains, cosine, sine, tag, *key_value_w.args()],
        [
            pltpu.VMEM((parts, shard, 2 * KW), BF),
            pltpu.SemaphoreType.DMA((key_value_w.copies,)),
        ],
        flops=4 * row_count * model_width * KW,
        nbytes=row_count * model_width * 4 + model_width * KW * 4,
        in_specs=[SMEM] + [VMEM] * 5 + [HBM] * key_value_w.count,
    )
    turns = [packed]
    while len(turns) < levels:
        turns.append(turn(turns[-1]))
    got_query = tie(near_query + rest_query, turns[-1])
    kept_kv = jnp.stack(turns, 0)
    kv = [kept_kv, swap_run(kept_kv, 1)]
    other_query = swap_run(jnp.concatenate(got_query, 0), 1)
    sent_wide = [columns_of([w_gate, w_up], mine ^ bit, ff_part) for bit in range(1, parts)]
    sent_wide = tie(sent_wide, *got_query)
    wide_hops = [hop(a, bit + 1) for bit, a in enumerate(sent_wide)]
    query_w = halves([w_query], got_query, [other_query], w_query.shape[1])
    query_raw = forward_mm(where, normed_one, query_w, parts)

    own_out, own_dm = at(w_out, core * half, half), cotangent.reshape(row_count, model_width)
    (own_out,), got_query = sync([own_out], got_query)
    all_out = lax.all_gather(own_out, "fsdp", axis=0, tiled=True)
    forward = [list(attend(0, query_raw, kv, tag, cosine, sine, tok_count))]
    wide_hops, forward[0], (own_dm,) = sync(wide_hops, forward[0], [own_dm])
    rings = [jnp.concatenate(wide_hops, 0)]
    moving = turn(rings[0])
    grad_y_low = own_dm
    near_dm = near_of(own_dm)
    for seq in range(1, seq_count):
        forward.append(
            list(
                attend(
                    seq, query_raw, kv, tag, cosine, sine, tok_count,
                    after=[rings[0], forward[-1][1]],
                )
            )
        )
    rot, attended, logs = [list(a) for a in zip(*forward)]
    (moving,), (attended[-1],), (all_out,) = sync([moving], [attended[-1]], [all_out])
    rings.append(moving)
    moving = turn(rings[-1])
    other_out = swap_run(all_out, 1)
    blocks = [(0, None, 0, 0, bit) for bit in range(1, parts)]
    blocks += [(1, None, 0, 1, bit) for bit in range(1, parts)]
    out_w = Pieces([w_out], [all_out, other_out], blocks, half, w_out.shape[1])
    attended = jnp.concatenate(attended, 0)
    inputs = x_low.astype(F32)
    residual = inputs + forward_mm(where, attended, out_w, parts)
    scale_two = rms_scale(residual)
    normed_two = (residual * scale_two * gain_two).astype(BF)
    (moving,), (normed_two,), near_dm = sync([moving], [normed_two], near_dm)
    near_normed = near_of(normed_two)
    far_dm = far_of(near_dm)
    all_dm = [grad_y_low] + near_dm + far_dm
    while len(rings) < levels - 1:
        rings.append(moving)
        moving = turn(rings[-1])
    near_normed, (moving,) = sync(near_normed, [moving])
    far_normed = far_of(near_normed)
    rings.append(moving)
    other_wide = swap_run(jnp.concatenate(rings, 0), 1)
    all_normed = [normed_two] + near_normed + far_normed
    cell = shard // runs
    blocks = []
    for back in range(levels):
        for bit in range(1, parts):
            blocks.append((back, (bit - 1) * cell, back, 0, bit))
            blocks.append((levels, (back * (parts - 1) + bit - 1) * cell, back, 1, bit))
    wide_w = Pieces([w_gate, w_up], rings + [other_wide], blocks, cell, 2 * ff_part, levels)

    if aligned:
        hidden_low, grad_wide_in, stacked, stacked_dm = feed(
            where, all_normed, all_dm, w_down, wide_w, parts
        )
    else:
        laid = lay_rows(wide_w)
        stacked = jnp.concatenate(all_normed, 0)
        stacked_dm = jnp.concatenate(all_dm, 0)
        gate_proj, up_proj = dot(stacked, laid[:, :ff_part]), dot(stacked, laid[:, ff_part:])
        sigmoid_gate = jax.nn.sigmoid(gate_proj)
        hidden_low = (gate_proj * sigmoid_gate * up_proj).astype(BF)
        grad_hidden = dot_cols(stacked_dm, w_down)
        grad_up_in = (grad_hidden * gate_proj * sigmoid_gate).astype(BF)
        slope = sigmoid_gate * (1.0 + gate_proj * (1.0 - sigmoid_gate))
        grad_wide_in = jnp.concatenate(
            [(grad_hidden * up_proj * slope).astype(BF), grad_up_in], 1
        )

    def blocks_of(total):
        return [total[b * half : (b + 1) * half] for b in range(parts)]

    def split(both, *counts):
        out = []
        for count in counts:
            out.append(both[:count])
            both = both[count:]
        return [*out, both]

    down_rows = ff_part // 2
    middle = model_width // 2

    def both_rows(done, first, cols, target, row=0):
        return [
            (done[0], first, cols, target, lambda m, k: (k * half + row, 0)),
            (done[1], first, cols, target, lambda m, k: ((1 - k) * half + row, 0)),
        ]

    def put(steps, outs):
        pieces, plan = [], []
        for piece, column, cols, target, spot, *span in steps:
            if not any(piece is p for p in pieces):
                pieces.append(piece)
            index = [piece is p for p in pieces].index(True)
            first, rows = span or (0, piece.shape[0])
            plan.append((index, first, column, rows, cols, target, spot))
        return place(where, pieces, plan, outs)

    full = (shard, parts * ff_part)

    def place_wide(wide_done):
        if not aligned:
            outs = [jnp.zeros(full, F32), jnp.zeros(full, F32)]
            for bit in range(parts):
                for side in range(2):
                    spot = ((core ^ side) * half, (mine ^ bit) * ff_part)
                    piece = wide_done[bit][side].astype(F32)
                    for number in range(2):
                        part = piece[:, number * ff_part : (number + 1) * ff_part]
                        outs[number] = lax.dynamic_update_slice(outs[number], part, spot)
            return outs
        steps = []
        for bit in range(parts):
            for side in range(2):
                for target in range(2):

                    def spot(m, k, bit=bit, side=side):
                        row = pl.multiple_of((k ^ side) * half, half)
                        return row, pl.multiple_of((m ^ bit) * ff_part, 128)

                    steps.append(
                        (wide_done[bit][side], target * ff_part, ff_part, target, spot)
                    )
        return put(steps, [full, full])

    def place_down(down_done):
        if not aligned:
            out = jnp.zeros((ff_part, model_width), F32)
            for number in range(2):
                for side in range(2):
                    spot = (number * down_rows, (core ^ side) * middle)
                    piece = down_done[number][side].astype(F32)
                    out = lax.dynamic_update_slice(out, piece, spot)
            return out
        steps = []
        for number in range(2):
            for side in range(2):

                def spot(m, k, number=number, side=side):
                    return number * down_rows, pl.multiple_of((k ^ side) * middle, 128)

                steps.append((down_done[number][side], 0, middle, 0, spot))
        return put(steps, [(ff_part, model_width)])[0]

    def sum_apart(arrays, flip):
        groups = [[2 * l + (k ^ flip) for l in range(levels)] for k in range(2)]
        return list(lax.psum(tuple(arrays), "ctx", axis_index_groups=groups))

    def pull(seq, number, after=()):
        heads = range(number * KVH // 2, (number + 1) * KVH // 2)
        after = list(after) + [a[0] for a in backward[-1:]]
        backward.append(
            attend_back(
                seq, heads, rot[seq], kv, tag, logs[seq], grad_attended, cosine, sine,
                tok_count, after=after,
            )
        )

    def sync_pulled(climbs, *groups):
        pulled, *rest = sync_climbs(climbs, backward[-1], *groups)
        backward[-1] = pulled
        return rest

    down_sent = dot_rows(hidden_low, at(stacked_dm, (1 - core) * middle, middle, 1)).astype(BF)
    (down_sent,), (hidden_low,) = sync([down_sent], [hidden_low])
    down_got = swap_run(down_sent, 1)
    down_kept = dot_rows(hidden_low, at(stacked_dm, core * middle, middle, 1)).astype(BF)
    down_pair = add(down_kept, down_got)
    down = [Climb(down_pair[i * down_rows : (i + 1) * down_rows]) for i in range(2)]
    moving = advance(down[:1])

    if aligned:
        back_blocks = back_mm(where, grad_wide_in, wide_w, parts, BF, parts, after=values(down))
    else:
        back_rows = dot_cols(grad_wide_in, laid).astype(BF)
        back_blocks = [back_rows[i * row_count : (i + 1) * row_count] for i in range(parts)]
    back_got = sum_first(back_blocks)
    wide_sent = grad_mm(
        where, stacked, grad_wide_in, 1, parts, after=back_blocks[:1]
    )
    wide_sent, back_got, moving = sync(wide_sent, back_got, moving)
    take(down[:1], moving)

    moving = advance(down)
    wide_got = swap_all(wide_sent)
    back_got = sum_second(back_blocks, back_got)
    wide_blocks = grad_mm(
        where, stacked, grad_wide_in, 0, parts, got=wide_got, after=values(down), outs=parts
    )
    back_got, wide_blocks, moving = sync(back_got, wide_blocks, moving)
    take(down, moving)

    moving = advance(down)
    wide_moved = [hop(a, bit + 1) for bit, a in enumerate(wide_blocks[1:])]
    grad_normed_two = sum_last(back_blocks, back_got)
    grad_y = grad_y_low.astype(F32)
    grad_res_norm, grad_gain_two = norm_back(grad_normed_two, residual, scale_two, gain_two)
    grad_residual = grad_y + grad_res_norm
    grad_proj = grad_residual.astype(BF)
    (grad_attended,) = back_mm(where, grad_proj, out_w, parts, BF)
    (grad_attended,), wide_moved[:1], moving = sync(
        [grad_attended], wide_moved[:1], moving
    )
    take(down, moving)

    wide_near = sum_apart(wide_blocks[:1] + wide_moved[:1], 1)
    moving = advance(down[1:])
    backward = []
    for seq in range(seq_count):
        for number in range(2):
            pull(seq, number, values(down) if seq == 0 else ())

    def lay(index):
        rows = [
            [backward[2 * seq + number][index] for number in range(2)]
            for seq in range(seq_count)
        ]
        if index == 0:
            return jnp.concatenate([jnp.concatenate(r, 1) for r in rows], 0)
        step = KW // 2
        keys = jnp.concatenate([jnp.concatenate([a[..., :step] for a in r], 2) for r in rows], 1)
        rest = jnp.concatenate([jnp.concatenate([a[..., step:] for a in r], 2) for r in rows], 1)
        return jnp.concatenate([keys, rest], 2)

    out_sent = grad_mm(
        where, attended, grad_proj, 1, parts, after=[backward[-1][0]], outs=2
    )
    grad_query_low = lay(0)
    query_sent = grad_mm(
        where, normed_one, grad_query_low, 1, parts, after=out_sent[:1], outs=2
    )
    (grad_normed_one,) = back_mm(
        where, grad_query_low, query_w, parts, F32, after=query_sent[:1]
    )
    mixed_blocks = mix(hidden_low, w_down, parts, after=[grad_normed_one])
    (
        out_sent, query_sent, wide_near, wide_moved[1:], (grad_normed_one,), moving, mixed_blocks
    ) = sync_pulled(
        [], out_sent, query_sent, wide_near, wide_moved[1:], [grad_normed_one], moving,
        mixed_blocks,
    )
    take(down[1:], moving)

    wide_far = sum_apart(wide_moved[1:], 0)
    other_dkv = swap_run(lay(2), 1)
    out_got = swap_all(out_sent)
    by_level = add(lay(1), other_dkv)
    kv_parts = []
    for step in range(1, levels):
        pairs = [(i, (i - step) % levels) for i in range(levels)]
        kv_parts.append(level_send(by_level[step], pairs))
    out_blocks = grad_mm(
        where, attended, grad_proj, 0, parts, got=out_got, after=[by_level], outs=parts
    )
    out_mid = sum_first(out_blocks)
    out_mid, kv_parts, query_sent = sync(out_mid, kv_parts, query_sent)

    query_got = swap_all(query_sent)
    out_end = sum_second(out_blocks, out_mid)
    grad_kv_low = call(
        kv_back_body,
        shape((row_count, 2 * KW), BF),
        [by_level[0], *kv_parts, cosine, sine],
        nbytes=row_count * KW * 4 * (levels + 1),
        after=out_blocks[:1],
    )
    (kv_sent,) = grad_mm(where, normed_one, grad_kv_low, 1, parts)
    query_blocks = grad_mm(
        where, normed_one, grad_query_low, 0, parts, got=query_got, after=[kv_sent], outs=parts
    )
    out_end, (kv_sent,), query_blocks = sync(out_end, [kv_sent], query_blocks)

    out_sum = sum_last(out_blocks, out_end).astype(BF)
    query_mid = sum_first(query_blocks)
    kv_got = swap_run(kv_sent, 1)
    (grad_normed_kv,) = back_mm(where, grad_kv_low, key_value_w, parts, F32, after=[kv_sent])
    (kv_pair,) = grad_mm(
        where, normed_one, grad_kv_low, 0, parts, got=[kv_got], after=[grad_normed_kv]
    )
    query_mid, (kv_pair,) = sync(query_mid, [kv_pair])
    query_end = sum_second(query_blocks, query_mid)
    grad_normed_one = grad_normed_one + grad_normed_kv
    scale_one = rms_scale(inputs)
    grad_in_norm, grad_gain_one = norm_back(grad_normed_one, inputs, scale_one, gain_one)
    grad_in = (grad_residual + grad_in_norm).reshape(seq_count, tok_count, model_width)
    gain_rows = jnp.stack([grad_gain_one, grad_gain_two], 0).astype(BF)
    gain_rows = gain_rows.reshape(2, parts, 2, half)
    gain_rows = jnp.concatenate(
        [lax.dynamic_slice(gain_rows, (0, mine ^ b, 0, 0), (2, 1, 2, half)) for b in range(parts)],
        1,
    )
    gain_sent = at(gain_rows, 1 - core, 1, 2).reshape(2, parts * half)
    gain_kept = at(gain_rows, core, 1, 2).reshape(2, parts * half)
    gain_cols = add(gain_kept, swap_run(gain_sent, 1)).T
    gain_cols = jnp.concatenate([gain_cols, jnp.zeros((parts * half, 126), BF)], 1)
    kv_blocks = blocks_of(jnp.concatenate([kv_pair, gain_cols], 1))
    query_end, kv_blocks, (grad_in,) = sync(query_end, kv_blocks, [grad_in])

    query_sum = sum_last(query_blocks, query_end).astype(BF)
    kv_mid = sum_first(kv_blocks)
    mixed_mid = sum_first(mixed_blocks)
    down_got = swap_all([complete(c).value for c in down])
    kv_mid, (query_sum,), down_got, mixed_mid = sync(kv_mid, [query_sum], down_got, mixed_mid)
    down_done = [[c.value, a] for c, a in zip(down, down_got)]
    kv_end = sum_second(kv_blocks, kv_mid)
    grad_down = place_down(down_done)
    kv_end, (grad_down,) = sync(kv_end, [grad_down])
    kv_sum = sum_last(kv_blocks, kv_end).astype(BF)

    wide_far, last, mixed_mid = sync(wide_far, [out_sum, query_sum, kv_sum], mixed_mid)
    last = sum_apart(last, 1)
    wide_done = [[a, swap_run(a, 1)] for a in wide_near + wide_far]
    mixed_end = sum_second(mixed_blocks, mixed_mid)
    grad_gate_w, grad_up_w = place_wide(wide_done)
    mixed_end, (grad_gate_w, grad_up_w) = sync(mixed_end, [grad_gate_w, grad_up_w])
    output = (residual + sum_last(mixed_blocks, mixed_end)).astype(BF)
    output = output.reshape(seq_count, tok_count, model_width)
    last, (output,) = sync(last, [output])
    out_done, query_done, kv_done = [[a, swap_run(a, 1)] for a in last]
    (grad_out_w,) = put(both_rows(out_done, 0, model_width, 0), [(shard, model_width)])
    grad_query_w, grad_key_w, grad_value_w, gain_out = put(
        both_rows(query_done, 0, model_width, 0)
        + both_rows(kv_done, 0, KW, 1)
        + both_rows(kv_done, KW, KW, 2)
        + both_rows(kv_done, 2 * KW, 128, 3),
        [(shard, model_width), (shard, KW), (shard, KW), (shard, 128)],
    )
    return (
        output,
        grad_in,
        gain_out[:, 0],
        grad_query_w,
        grad_key_w,
        grad_value_w,
        grad_out_w,
        gain_out[:, 1],
        grad_gate_w,
        grad_up_w,
        grad_down,
    )


def solution(mesh):
    placed = (
        P("fsdp", "ctx", None),
        P("fsdp", "ctx"),
        P("fsdp", "ctx", None),
        P("fsdp"),
        P("fsdp", None),
        P("fsdp", None),
        P("fsdp", None),
        P("fsdp", None),
        P("fsdp"),
        P("fsdp", None),
        P("fsdp", None),
        P("fsdp", None),
    )
    return jax.shard_map(
        on_device,
        mesh=mesh,
        in_specs=placed,
        out_specs=(
            P("fsdp", "ctx", None),
            P("fsdp", "ctx", None),
            P("fsdp"),
            P("fsdp", None),
            P("fsdp", None),
            P("fsdp", None),
            P("fsdp", None),
            P("fsdp"),
            P("fsdp", None),
            P("fsdp", None),
            P("fsdp", None),
        ),
        check_vma=False,
    )
```
